32 devices in a mesh: tm: 8 (over z, core), freq: 4 (over y, x).
Axes of the slice: x: 2, y: 2, z: 4, core: 2. Of those that a mesh axis runs over, the one named last changes fastest.
Arguments:
- tokens: bfloat16 [128, 64, 1024], P('tm', 'freq'), may hold values from -16 to 16
- w_query: bfloat16 [1024, 1024], replicated, may hold values from -1 to 1
- w_key: bfloat16 [1024, 1024], replicated, may hold values from -1 to 1
- w_value: bfloat16 [1024, 1024], replicated, may hold values from -0.1875 to 0.1875
- w_out: bfloat16 [1024, 1024], replicated, may hold values from -0.75 to 0.75
- d_out: bfloat16 [128, 64, 1024], P('tm', 'freq'), may hold values from -6 to 6
Outputs:
- output: bfloat16 [128, 64, 1024], P('tm', 'freq')
- input_grad: bfloat16 [128, 64, 1024], P('tm', 'freq')
- weight_grads: float32 [1024, 4, 1024], P(('tm', 'freq'))
The draws below stay inside these ranges and needn't reach their ends.
All inputs are finite; a program needn't handle non-finite values.
Results may differ from the reference program's by a relative error of at most 0.0093.
Values may be sent and summed in bfloat16 or wider, within the bound.
A program may use at most 256 MiB of HBM per device.

```python
import math
import jax
import jax.numpy as jnp
from jax import lax

D = 1024
HEADS = 8
TIME = 128
FREQ = 64


def draw_tokens(key, part):
    base_key = jax.random.fold_in(key, 101)
    scale_key = jax.random.fold_in(key, 102)
    feature_scale = 0.5 * jnp.exp(jax.random.uniform(scale_key, (D,), jnp.float32, 0.0, math.log(10.0)))
    field = jax.random.normal(base_key, (TIME, FREQ, D), jnp.float32) * feature_scale
    return jnp.clip(field, -16.0, 16.0).astype(jnp.bfloat16)


def paired_weight(key, which):
    own = jax.random.normal(jax.random.fold_in(key, 202 + which), (D, D), jnp.float32)
    matrix = own
    return jnp.clip(matrix * D ** (-0.5), -1.0, 1.0).astype(jnp.bfloat16)


def draw_w_query(key, part):
    return paired_weight(key, 0)


def draw_w_key(key, part):
    return paired_weight(key, 1)


def block_scale(own_key, dims, split, least, largest):
    def one(position, parts):
        steps = jax.random.uniform(jax.random.fold_in(jax.random.fold_in(own_key, 6), position), (parts,), jnp.float32, least / len(split), largest / len(split))
        return jnp.repeat(jnp.exp(steps), dims[position] // parts).reshape((-1,) + (1,) * (len(dims) - position - 1))

    gain = one(*split[0])
    for cut in split[1:]:
        gain = gain * one(*cut)
    return gain


def centred(rng, extent, width, most, split=(), kind=jnp.bfloat16):
    drawn = jax.random.normal(rng, extent, jnp.float32) * width
    if len(split) > 0:
        drawn = block_scale(rng, extent, split, -0.22, 0.18) * drawn
    return jnp.clip(drawn, min=-most, max=most).astype(kind)


def setup_inputs(seed: int = 0) -> dict:
    arg_keys = jax.random.split(jax.random.key(seed), 7)
    tokens = draw_tokens(jax.random.fold_in(arg_keys[6], 71), 0)
    w_query = draw_w_query(jax.random.fold_in(arg_keys[6], 71), 0)
    w_key = draw_w_key(jax.random.fold_in(arg_keys[6], 71), 0)
    w_value = centred(arg_keys[3], (D, D), D ** -0.5, 0.1875)
    w_out = centred(arg_keys[4], (D, D), (D // 16) ** -0.5, 0.75)
    d_out = centred(arg_keys[5], (TIME, FREQ, D), 1.0, 6.0, ((0, 8), (1, 4)))
    return dict(tokens=tokens, w_query=w_query, w_key=w_key, w_value=w_value, w_out=w_out, d_out=d_out)


window_reach = 6
tile_edge = 8
span_edge = 20
norm_eps = 1e-05
far_value = -1e+30

def mix(form, left_operand, right_operand):
    return jnp.einsum(form, left_operand.astype(jnp.float32), right_operand.astype(jnp.float32))

def window_mask():
    query_pos = jnp.arange(tile_edge * tile_edge)
    key_pos = jnp.arange(span_edge * span_edge)
    rise_rows = (key_pos // span_edge)[None, :] - (query_pos // tile_edge)[:, None]
    rise_cols = (key_pos % span_edge)[None, :] - (query_pos % tile_edge)[:, None]
    return (rise_rows >= 0) & (rise_rows <= 2 * window_reach) & (rise_cols >= 0) & (rise_cols <= 2 * window_reach)

def pack_tiles(field_map):
    row_total, col_total = (field_map.shape[0], field_map.shape[1])
    trailing = field_map.shape[2:]
    shaped = field_map.reshape((row_total // tile_edge, tile_edge, col_total // tile_edge, tile_edge) + trailing)
    axes_order = (0, 2, 1, 3) + tuple(range(4, shaped.ndim))
    return shaped.transpose(axes_order).reshape((row_total // tile_edge * (col_total // tile_edge), tile_edge * tile_edge) + trailing)

def unpack_tiles(tile_stack, row_total, col_total):
    trailing = tile_stack.shape[2:]
    shaped = tile_stack.reshape((row_total // tile_edge, col_total // tile_edge, tile_edge, tile_edge) + trailing)
    axes_order = (0, 2, 1, 3) + tuple(range(4, shaped.ndim))
    return shaped.transpose(axes_order).reshape((row_total, col_total) + trailing)

def spread_tiles(field_map, row_total, col_total):
    trailing = field_map.shape[2:]
    tile_rows = row_total // tile_edge
    tile_cols = col_total // tile_edge
    row_index = (tile_edge * jnp.arange(tile_rows))[:, None] + jnp.arange(span_edge)[None, :]
    col_index = (tile_edge * jnp.arange(tile_cols))[:, None] + jnp.arange(span_edge)[None, :]
    picked = jnp.take(field_map, row_index, axis=0)
    picked = jnp.take(picked, col_index, axis=2)
    axes_order = (0, 2, 1, 3) + tuple(range(4, picked.ndim))
    return picked.transpose(axes_order).reshape((tile_rows * tile_cols, span_edge * span_edge) + trailing)

def group_size(tile_count):
    best_width = 1
    for candidate in range(1, 9):
        if tile_count % candidate == 0:
            best_width = candidate
    return best_width

def over_groups(group_func, members):
    tile_count = members[0].shape[0]
    best_width = group_size(tile_count)
    grouped = tuple((member.reshape((tile_count // best_width, best_width) + member.shape[1:]) for member in members))
    results = lax.map(lambda group_parts: group_func(*group_parts), grouped)
    return tuple((member.reshape((tile_count,) + member.shape[2:]) for member in results))

def attend_forward(query_map, key_map, value_map, key_ok, head_count):
    row_total, col_total, model_width = query_map.shape
    head_dim = model_width // head_count
    score_scale = 1.0 / math.sqrt(head_dim)
    inside = window_mask()
    q_tiles = pack_tiles(query_map).reshape(-1, tile_edge * tile_edge, head_count, head_dim)
    k_tiles = spread_tiles(key_map, row_total, col_total).reshape(-1, span_edge * span_edge, head_count, head_dim)
    v_tiles = spread_tiles(value_map, row_total, col_total).reshape(-1, span_edge * span_edge, head_count, head_dim)
    ok_tiles = spread_tiles(key_ok, row_total, col_total)

    def one_group(q_part, k_part, v_part, ok_part):
        allowed = inside[None, None] & (ok_part[:, None, None, :] > 0.5)
        scores = mix('nqhd,nkhd->nhqk', q_part, k_part) * score_scale
        scores = jnp.where(allowed, scores, far_value)
        row_max = lax.optimization_barrier(jnp.max(scores, axis=-1, keepdims=True))
        log_total = row_max + jnp.log(lax.optimization_barrier(jnp.sum(jnp.exp(scores - row_max), axis=-1, keepdims=True)))
        soft_weights = jnp.where(allowed, jnp.exp(scores - log_total), 0.0)
        attended = mix('nhqk,nkhd->nqhd', soft_weights.astype(jnp.bfloat16), v_part)
        return (attended, log_total[..., 0])
    attended, log_total = over_groups(one_group, (q_tiles, k_tiles, v_tiles, ok_tiles))
    attended = unpack_tiles(attended.reshape(-1, tile_edge * tile_edge, model_width), row_total, col_total)
    log_total = unpack_tiles(log_total.transpose(0, 2, 1), row_total, col_total)
    return (attended, log_total)

def attend_query_grad(query_map, key_map, value_map, key_ok, grad_map, head_count):
    row_total, col_total, model_width = query_map.shape
    head_dim = model_width // head_count
    score_scale = 1.0 / math.sqrt(head_dim)
    inside = window_mask()
    q_tiles = pack_tiles(query_map).reshape(-1, tile_edge * tile_edge, head_count, head_dim)
    g_tiles = pack_tiles(grad_map).reshape(-1, tile_edge * tile_edge, head_count, head_dim)
    k_tiles = spread_tiles(key_map, row_total, col_total).reshape(-1, span_edge * span_edge, head_count, head_dim)
    v_tiles = spread_tiles(value_map, row_total, col_total).reshape(-1, span_edge * span_edge, head_count, head_dim)
    ok_tiles = spread_tiles(key_ok, row_total, col_total)

    def one_group(q_part, g_part, k_part, v_part, ok_part):
        allowed = inside[None, None] & (ok_part[:, None, None, :] > 0.5)
        scores = mix('nqhd,nkhd->nhqk', q_part, k_part) * score_scale
        scores = jnp.where(allowed, scores, far_value)
        row_max = lax.optimization_barrier(jnp.max(scores, axis=-1, keepdims=True))
        log_total = row_max + jnp.log(lax.optimization_barrier(jnp.sum(jnp.exp(scores - row_max), axis=-1, keepdims=True)))
        soft_weights = jnp.where(allowed, jnp.exp(scores - log_total), 0.0)
        grad_probs = mix('nqhd,nkhd->nhqk', g_part, v_part)
        spread = lax.optimization_barrier(jnp.sum(soft_weights * grad_probs, axis=-1, keepdims=True))
        grad_scores = (soft_weights * (grad_probs - spread) * score_scale).astype(jnp.bfloat16)
        grad_query = mix('nhqk,nkhd->nqhd', grad_scores, k_part)
        return (grad_query, log_total[..., 0], spread[..., 0])
    grad_query, log_total, spread = over_groups(one_group, (q_tiles, g_tiles, k_tiles, v_tiles, ok_tiles))
    grad_query = unpack_tiles(grad_query.reshape(-1, tile_edge * tile_edge, model_width), row_total, col_total)
    log_total = unpack_tiles(log_total.transpose(0, 2, 1), row_total, col_total)
    spread = unpack_tiles(spread.transpose(0, 2, 1), row_total, col_total)
    return (grad_query, log_total, spread)

def attend_key_grad(key_map, value_map, query_map, grad_map, log_total, spread, head_count):
    row_total, col_total, model_width = key_map.shape
    head_dim = model_width // head_count
    score_scale = 1.0 / math.sqrt(head_dim)
    inside = window_mask()
    k_tiles = pack_tiles(key_map).reshape(-1, tile_edge * tile_edge, head_count, head_dim)
    v_tiles = pack_tiles(value_map).reshape(-1, tile_edge * tile_edge, head_count, head_dim)
    q_tiles = spread_tiles(query_map, row_total, col_total).reshape(-1, span_edge * span_edge, head_count, head_dim)
    g_tiles = spread_tiles(grad_map, row_total, col_total).reshape(-1, span_edge * span_edge, head_count, head_dim)
    l_tiles = spread_tiles(log_total, row_total, col_total).transpose(0, 2, 1)
    s_tiles = spread_tiles(spread, row_total, col_total).transpose(0, 2, 1)

    def one_group(k_part, v_part, q_part, g_part, l_part, s_part):
        scores = mix('nkhd,nqhd->nhkq', k_part, q_part) * score_scale
        soft_weights = jnp.where(inside[None, None], jnp.exp(scores - l_part[:, :, None, :]), 0.0)
        grad_probs = mix('nkhd,nqhd->nhkq', v_part, g_part)
        grad_scores = (soft_weights * (grad_probs - s_part[:, :, None, :]) * score_scale).astype(jnp.bfloat16)
        grad_keys = mix('nhkq,nqhd->nkhd', grad_scores, q_part)
        grad_values = mix('nhkq,nqhd->nkhd', soft_weights.astype(jnp.bfloat16), g_part)
        return (grad_keys, grad_values)
    grad_keys, grad_values = over_groups(one_group, (k_tiles, v_tiles, q_tiles, g_tiles, l_tiles, s_tiles))
    grad_keys = unpack_tiles(grad_keys.reshape(-1, tile_edge * tile_edge, model_width), row_total, col_total)
    grad_values = unpack_tiles(grad_values.reshape(-1, tile_edge * tile_edge, model_width), row_total, col_total)
    return (grad_keys, grad_values)

def layer_norm(flat_rows):
    wide_values = flat_rows.astype(jnp.float32)
    center = lax.optimization_barrier(jnp.mean(wide_values, axis=-1, keepdims=True))
    shifted = wide_values - center
    inverse = lax.rsqrt(lax.optimization_barrier(jnp.mean(shifted * shifted, axis=-1, keepdims=True)) + norm_eps)
    return (shifted * inverse, inverse)

def pad_map(field_map, margin):
    return jnp.pad(field_map, ((margin, margin), (margin, margin)) + ((0, 0),) * (field_map.ndim - 2))

def reference(tokens, w_query, w_key, w_value, w_out, d_out):
    time_all, freq_all, model_width = tokens.shape
    flat_rows = tokens.reshape(-1, model_width)
    normed, inverse = layer_norm(flat_rows)
    hidden = normed.astype(jnp.bfloat16)
    query_rows = jnp.dot(hidden, w_query, preferred_element_type=jnp.float32).astype(jnp.bfloat16)
    key_rows = jnp.dot(hidden, w_key, preferred_element_type=jnp.float32).astype(jnp.bfloat16)
    value_rows = jnp.dot(hidden, w_value, preferred_element_type=jnp.float32).astype(jnp.bfloat16)
    query_map = query_rows.reshape(time_all, freq_all, model_width)
    key_pad = pad_map(key_rows.reshape(time_all, freq_all, model_width), window_reach)
    value_pad = pad_map(value_rows.reshape(time_all, freq_all, model_width), window_reach)
    ok_pad = pad_map(jnp.ones((time_all, freq_all), jnp.float32), window_reach)
    band_ids = jnp.arange(time_all // tile_edge, dtype=jnp.int32)

    def forward_band(band):
        row_start = (band * tile_edge).astype(jnp.int32)
        q_band = lax.dynamic_slice_in_dim(query_map, row_start, tile_edge, 0)
        k_band = lax.dynamic_slice_in_dim(key_pad, row_start, span_edge, 0)
        v_band = lax.dynamic_slice_in_dim(value_pad, row_start, span_edge, 0)
        ok_band = lax.dynamic_slice_in_dim(ok_pad, row_start, span_edge, 0)
        attended, unused = attend_forward(q_band, k_band, v_band, ok_band, HEADS)
        return attended.astype(jnp.bfloat16)
    attended_rows = lax.map(forward_band, band_ids).reshape(-1, model_width)
    output = (flat_rows.astype(jnp.float32) + jnp.dot(attended_rows, w_out, preferred_element_type=jnp.float32)).astype(jnp.bfloat16)
    grad_flat = d_out.reshape(-1, model_width)
    grad_att = jnp.dot(grad_flat, w_out.T, preferred_element_type=jnp.float32).astype(jnp.bfloat16)
    grad_map = grad_att.reshape(time_all, freq_all, model_width)

    def query_band(band):
        row_start = (band * tile_edge).astype(jnp.int32)
        q_band = lax.dynamic_slice_in_dim(query_map, row_start, tile_edge, 0)
        g_band = lax.dynamic_slice_in_dim(grad_map, row_start, tile_edge, 0)
        k_band = lax.dynamic_slice_in_dim(key_pad, row_start, span_edge, 0)
        v_band = lax.dynamic_slice_in_dim(value_pad, row_start, span_edge, 0)
        ok_band = lax.dynamic_slice_in_dim(ok_pad, row_start, span_edge, 0)
        grad_query, log_total, spread = attend_query_grad(q_band, k_band, v_band, ok_band, g_band, HEADS)
        return (grad_query.astype(jnp.bfloat16), log_total, spread)
    grad_query, log_total, spread = lax.map(query_band, band_ids)
    grad_query = grad_query.reshape(-1, model_width)
    log_pad = pad_map(log_total.reshape(time_all, freq_all, -1), window_reach)
    spread_pad = pad_map(spread.reshape(time_all, freq_all, -1), window_reach)
    query_pad = pad_map(query_map, window_reach)
    grad_pad = pad_map(grad_map, window_reach)
    key_map = key_rows.reshape(time_all, freq_all, model_width)
    value_map = value_rows.reshape(time_all, freq_all, model_width)

    def key_band(band):
        row_start = (band * tile_edge).astype(jnp.int32)
        k_band = lax.dynamic_slice_in_dim(key_map, row_start, tile_edge, 0)
        v_band = lax.dynamic_slice_in_dim(value_map, row_start, tile_edge, 0)
        q_band = lax.dynamic_slice_in_dim(query_pad, row_start, span_edge, 0)
        g_band = lax.dynamic_slice_in_dim(grad_pad, row_start, span_edge, 0)
        l_band = lax.dynamic_slice_in_dim(log_pad, row_start, span_edge, 0)
        s_band = lax.dynamic_slice_in_dim(spread_pad, row_start, span_edge, 0)
        grad_keys, grad_values = attend_key_grad(k_band, v_band, q_band, g_band, l_band, s_band, HEADS)
        return (grad_keys.astype(jnp.bfloat16), grad_values.astype(jnp.bfloat16))
    grad_keys, grad_values = lax.map(key_band, band_ids)
    grad_keys = grad_keys.reshape(-1, model_width)
    grad_values = grad_values.reshape(-1, model_width)
    weight_grads = jnp.stack([jnp.dot(hidden.T, grad_query, preferred_element_type=jnp.float32), jnp.dot(hidden.T, grad_keys, preferred_element_type=jnp.float32), jnp.dot(hidden.T, grad_values, preferred_element_type=jnp.float32), jnp.dot(attended_rows.T, grad_flat, preferred_element_type=jnp.float32)], axis=1)
    grad_hidden = jnp.dot(grad_query, w_query.T, preferred_element_type=jnp.float32)
    grad_hidden = grad_hidden + jnp.dot(grad_keys, w_key.T, preferred_element_type=jnp.float32)
    grad_hidden = grad_hidden + jnp.dot(grad_values, w_value.T, preferred_element_type=jnp.float32)
    center_grad = lax.optimization_barrier(jnp.mean(grad_hidden, axis=-1, keepdims=True))
    along = lax.optimization_barrier(jnp.mean(grad_hidden * normed, axis=-1, keepdims=True))
    input_grad = (grad_flat.astype(jnp.float32) + (grad_hidden - center_grad - normed * along) * inverse).astype(jnp.bfloat16)
    return (output.reshape(time_all, freq_all, model_width), input_grad.reshape(time_all, freq_all, model_width), weight_grads)
```

```python
import functools
import math

import jax
import jax.numpy as jnp
from jax import lax
from jax.experimental import pallas as pl
from jax.experimental.pallas import tpu as pltpu
from jax.sharding import PartitionSpec as P

HEADS = 8
REACH = 6
EPS = 1e-05
FAR = -1e30
MESH = pl.DeviceIdType.MESH
F32 = jnp.float32
BF16 = jnp.bfloat16


def nn(a, b):
    return lax.dot_general(a, b, (((1,), (0,)), ((), ())), preferred_element_type=F32)


def nt(a, b):
    return lax.dot_general(a, b, (((1,), (1,)), ((), ())), preferred_element_type=F32)


def query_kernel(scale, n_q, n_k, step, q_ref, g_ref, k_ref, v_ref, bias_ref, att_ref, gq_ref, stat_ref):
    for half in range(2):
        rows = slice(half * n_q, (half + 1) * n_q)
        cols = slice(half * step, half * step + n_k)
        k = k_ref[cols, :]
        v = v_ref[cols, :]
        s = nt(q_ref[rows, :], k) * scale + bias_ref[half]
        top = jnp.max(s, axis=-1, keepdims=True)
        e = jnp.exp(s - top)
        total = jnp.sum(e, axis=-1, keepdims=True)
        probs = e * (1.0 / total)
        att_ref[rows, :] = nn(probs.astype(BF16), v).astype(BF16)
        gp = nt(g_ref[rows, :], v)
        spread = jnp.sum(probs * gp, axis=-1, keepdims=True)
        gs = (probs * (gp - spread) * scale).astype(BF16)
        gq_ref[rows, :] = nn(gs, k).astype(BF16)
        lane = lax.broadcasted_iota(jnp.int32, (n_q, 128), 1)
        both = jnp.where(lane == 0, top + jnp.log(total), spread)
        stat_ref[0, :, rows] = both.T[0:8, :]


def key_kernel(scale, n_q, n_k, step, k_ref, v_ref, q_ref, g_ref, bias_ref, stat_ref, gk_ref, gv_ref):
    for half in range(2):
        rows = slice(half * n_q, (half + 1) * n_q)
        cols = slice(half * step, half * step + n_k)
        q = q_ref[cols, :]
        g = g_ref[cols, :]
        s = nt(k_ref[rows, :], q) * scale + bias_ref[half]
        probs = jnp.exp(s - stat_ref[0, 0:1, cols])
        gv_ref[rows, :] = nn(probs.astype(BF16), g).astype(BF16)
        gp = nt(v_ref[rows, :], g)
        gs = (probs * (gp - stat_ref[0, 1:2, cols]) * scale).astype(BF16)
        gk_ref[rows, :] = nn(gs, q).astype(BF16)


def head_spec(rows, width):
    return pl.BlockSpec((rows, width), lambda h: (0, h))


def attention_calls(n_own, n_ext, width, model, half_q, half_k, step):
    scale = 1.0 / math.sqrt(width)
    own, ext = head_spec(n_own, width), head_spec(n_ext, width)
    bias = pl.BlockSpec((2, half_q, half_k), lambda h: (0, 0, 0))
    big = jax.ShapeDtypeStruct((n_own, model), BF16)
    params = pltpu.CompilerParams(vmem_limit_bytes=32 * 1024 * 1024)
    first = pl.pallas_call(
        functools.partial(query_kernel, scale, half_q, half_k, step),
        grid=(HEADS,),
        in_specs=[own, own, ext, ext, bias],
        out_specs=[own, own, pl.BlockSpec((1, 8, n_own), lambda h: (h, 0, 0))],
        out_shape=[big, big, jax.ShapeDtypeStruct((HEADS, 8, n_own), F32)],
        compiler_params=params,
        cost_estimate=pl.CostEstimate(
            flops=10 * n_own * half_k * model, bytes_accessed=4 * n_ext * model, transcendentals=0
        ),
    )
    second = pl.pallas_call(
        functools.partial(key_kernel, scale, half_q, half_k, step),
        grid=(HEADS,),
        in_specs=[own, own, ext, ext, bias, pl.BlockSpec((1, 2, n_ext), lambda h: (h, 0, 0))],
        out_specs=[own, own],
        out_shape=[big, big],
        compiler_params=params,
        cost_estimate=pl.CostEstimate(
            flops=8 * n_own * half_k * model, bytes_accessed=4 * n_ext * model, transcendentals=0
        ),
    )
    return first, second


def log2(n):
    return n.bit_length() - 1


def axis_orders(t_size, f_size):
    rest = [("freq", b) for b in range(log2(f_size))] + [("tm", b) for b in range(1, log2(t_size))]
    head, last = rest[:-1], rest[-1:]
    turns = [head[i:] + head[:i] for i in (2, 1, 0)] + [[head[1], head[0]] + head[2:]]
    return [[("tm", 0)] + turn + last for turn in turns]


def scatter_kernel(orders, sizes, *refs):
    n_mat = len(orders)
    n_st = len(orders[0])
    lefts = refs[:n_mat]
    rights = refs[n_mat : 2 * n_mat]
    out_ref = refs[2 * n_mat]
    total = refs[2 * n_mat + 1]
    sends = refs[2 * n_mat + 2 : 2 * n_mat + 2 + n_st]
    lands = refs[2 * n_mat + 2 + n_st : 2 * n_mat + 2 + 2 * n_st]
    send_sem, recv_sem = refs[-2:]
    tm, fq = lax.axis_index("tm"), lax.axis_index("freq")

    def bit(dim):
        axis, b = dim
        return ((tm if axis == "tm" else fq) // (1 << b)) % 2

    def partner(dim):
        axis, b = dim
        move = (1 - 2 * bit(dim)) * (1 << b)
        return (tm + move, fq) if axis == "tm" else (tm, fq + move)

    barrier = pltpu.get_barrier_semaphore()
    for dim in orders[0]:
        pl.semaphore_signal(barrier, inc=1, device_id=partner(dim), device_id_type=MESH)
    pl.semaphore_wait(barrier, n_st)

    def copy(m, st):
        return pltpu.make_async_remote_copy(
            src_ref=sends[st].at[m],
            dst_ref=lands[st].at[m],
            send_sem=send_sem.at[m, st],
            recv_sem=recv_sem.at[m, st],
            device_id=partner(orders[m][st]),
            device_id_type=MESH,
        )

    turn = list(range(n_mat - 1, -1, -1))
    half = sizes[0]
    for m in turn:
        theirs = pl.multiple_of((1 - bit(orders[m][0])) * half, half)
        sends[0][m] = nn(lefts[m][pl.ds(theirs, half), :], rights[m][...]).astype(BF16)
        copy(m, 0).start()
    for m in turn:
        mine = pl.multiple_of(bit(orders[m][0]) * half, half)
        total[m] = nn(lefts[m][pl.ds(mine, half), :], rights[m][...])
    base = [0] * n_mat
    for st in range(1, n_st):
        half = sizes[st]
        for m in turn:
            copy(m, st - 1).wait()
            b = bit(orders[m][st])
            theirs, mine = (1 - b) * half, b * half
            if half >= 16:
                theirs, mine = pl.multiple_of(theirs, half), pl.multiple_of(mine, half)
                there = pl.multiple_of(base[m] + theirs, half)
                here = pl.multiple_of(base[m] + mine, half)
                away = total[m, pl.ds(there, half), :] + lands[st - 1][m, pl.ds(theirs, half), :].astype(F32)
                sends[st][m] = away.astype(BF16)
                copy(m, st).start()
                total[m, pl.ds(here, half), :] += lands[st - 1][m, pl.ds(mine, half), :].astype(F32)
            else:
                start = pl.multiple_of(base[m], 2 * half)
                both = total[m, pl.ds(start, 2 * half), :] + lands[st - 1][m].astype(F32)
                low, high = both[:half], both[half:]
                away = jnp.where(b == 0, high, low)
                sends[st][m] = jnp.concatenate([away, away], axis=0).astype(BF16)
                copy(m, st).start()
                here = pl.multiple_of(base[m] + mine, half)
                total[m, pl.ds(here, half), :] = jnp.where(b == 0, low, high)
            base[m] = here
    half = sizes[-1]
    for m in turn:
        copy(m, n_st - 1).wait()
        out_ref[m] = total[m, pl.ds(base[m], half), :] + lands[-1][m].astype(F32)[0:half]


def scatter_sum(lefts, rights, t_size, f_size):
    n_dev = t_size * f_size
    n_st = log2(n_dev)
    orders = axis_orders(t_size, f_size)
    tokens, model = lefts[0].shape
    rows = model // n_dev
    sizes = [model >> (s + 1) for s in range(n_st)]
    flipped = []
    for left, order in zip(lefts, orders):
        place = [
            log2(t_size) - 1 - b if axis == "tm" else log2(t_size) + log2(f_size) - 1 - b for axis, b in order
        ]
        cube = left.T.reshape((2,) * n_st + (rows, tokens))
        flipped.append(cube.transpose(place + [n_st, n_st + 1]).reshape(model, tokens))
    n_mat = len(orders)
    blocks = [(n_mat, max(s, 16), model) for s in sizes]
    vm = pl.BlockSpec(memory_space=pltpu.VMEM)
    return pl.pallas_call(
        functools.partial(scatter_kernel, orders, sizes),
        out_shape=jax.ShapeDtypeStruct((n_mat, rows, model), F32),
        in_specs=[vm] * (2 * n_mat),
        out_specs=vm,
        scratch_shapes=[pltpu.VMEM((n_mat, sizes[0], model), F32)]
        + [pltpu.VMEM(b, BF16) for b in blocks]
        + [pltpu.VMEM(b, BF16) for b in blocks]
        + [pltpu.SemaphoreType.DMA((n_mat, n_st)), pltpu.SemaphoreType.DMA((n_mat, n_st))],
        compiler_params=pltpu.CompilerParams(
            collective_id=1, has_side_effects=True, vmem_limit_bytes=56 * 1024 * 1024
        ),
        cost_estimate=pl.CostEstimate(
            flops=2 * n_mat * tokens * model * model, bytes_accessed=4 * tokens * model, transcendentals=0
        ),
    )(*flipped, *rights)


def extended(array, sides):
    for axis, dim in sides:
        size, length = lax.axis_size(axis), array.shape[dim]
        up = [(i, i + 1) for i in range(size - 1)]
        down = [(j, i) for i, j in up]
        last = lax.slice_in_dim(array, length - REACH, length, axis=dim)
        leading = lax.slice_in_dim(array, 0, REACH, axis=dim)
        before = lax.ppermute(last, axis, up)
        after = lax.ppermute(leading, axis, down)
        array = jnp.concatenate([before, array, after], axis=dim)
    return array


def layer_norm(flat_rows):
    wide = flat_rows.astype(F32)
    center = jnp.mean(wide, axis=-1, keepdims=True)
    shifted = wide - center
    inverse = lax.rsqrt(jnp.mean(shifted * shifted, axis=-1, keepdims=True) + EPS)
    return shifted * inverse, inverse


def window_bias(n_t, n_f, wide):
    half_t = n_t // 2
    span = half_t + 2 * REACH
    t0 = lax.axis_index("tm") * n_t
    f0 = lax.axis_index("freq") * n_f
    half = jnp.arange(2)[:, None, None]
    own = jnp.arange(half_t * n_f)[None, :, None]
    key = jnp.arange(span * wide)[None, None, :]
    own_t, own_f = own // n_f, own % n_f
    key_t, key_f = key // wide - REACH, key % wide - REACH
    at_t = t0 + half * half_t + key_t
    at_f = f0 + key_f
    ok = (
        (jnp.abs(key_t - own_t) <= REACH)
        & (jnp.abs(key_f - own_f) <= REACH)
        & (at_t >= 0)
        & (at_t < n_t * lax.axis_size("tm"))
        & (at_f >= 0)
        & (at_f < n_f * lax.axis_size("freq"))
    )
    return jnp.where(ok, 0.0, FAR).astype(F32)


def local(tokens, w_query, w_key, w_value, w_out, d_out):
    n_t, n_f, model = tokens.shape
    n_own = n_t * n_f
    width = model // HEADS
    wide = -(-(n_f + 2 * REACH) // 16) * 16
    tall = n_t + 2 * REACH
    n_ext = tall * wide
    half_t = n_t // 2

    def pad(a):
        return jnp.pad(a, ((0, 0),) * (a.ndim - 1) + ((0, wide - a.shape[-1]),))

    near = extended(jnp.stack([tokens, d_out]), (("tm", 1), ("freq", 2)))
    near = jnp.pad(near, ((0, 0), (0, 0), (0, wide - near.shape[2]), (0, 0)))
    near_tokens = near[0].reshape(n_ext, model)
    near_grad = near[1].reshape(n_ext, model)

    flat = tokens.reshape(n_own, model)
    normed, inverse = layer_norm(flat)
    hidden = normed.astype(BF16)
    near_hidden = layer_norm(near_tokens)[0].astype(BF16)
    grad_flat = d_out.reshape(n_own, model)

    def project(a, w):
        return jnp.dot(a, w, preferred_element_type=F32).astype(BF16)

    query, key, value = project(hidden, w_query), project(hidden, w_key), project(hidden, w_value)
    grad_att = nt(grad_flat, w_out).astype(BF16)
    near_key, near_value = project(near_hidden, w_key), project(near_hidden, w_value)
    near_query = project(near_hidden, w_query)
    near_gatt = nt(near_grad, w_out).astype(BF16)

    bias = window_bias(n_t, n_f, wide)
    first, second = attention_calls(
        n_own, n_ext, width, model, half_t * n_f, (half_t + 2 * REACH) * wide, half_t * wide
    )
    attended, grad_query, stats = first(query, grad_att, near_key, near_value, bias)
    near_stats = extended(stats[:, :2].reshape(HEADS, 2, n_t, n_f), (("tm", 2), ("freq", 3)))
    near_stats = pad(near_stats).reshape(HEADS, 2, n_ext)
    output = (flat.astype(F32) + nn(attended, w_out)).astype(BF16)
    grad_key, grad_value = second(key, value, near_query, near_gatt, bias, near_stats)

    weight_grads = scatter_sum(
        [hidden, hidden, hidden, attended],
        [grad_query, grad_key, grad_value, grad_flat],
        lax.axis_size("tm"),
        lax.axis_size("freq"),
    ).transpose(1, 0, 2)

    grad_hidden = nt(grad_query, w_query) + nt(grad_key, w_key) + nt(grad_value, w_value)
    center = jnp.mean(grad_hidden, axis=-1, keepdims=True)
    along = jnp.mean(grad_hidden * normed, axis=-1, keepdims=True)
    input_grad = (grad_flat.astype(F32) + (grad_hidden - center - normed * along) * inverse).astype(BF16)
    return output.reshape(n_t, n_f, model), input_grad.reshape(n_t, n_f, model), weight_grads


def solution(mesh):
    tile = P("tm", "freq", None)
    in_specs = (tile, P(), P(), P(), P(), tile)
    out_specs = (tile, tile, P(("tm", "freq"), None, None))
    return jax.shard_map(local, mesh=mesh, in_specs=in_specs, out_specs=out_specs, check_vma=False)
```

```python
import functools
import math

import jax
import jax.numpy as jnp
from jax import lax
from jax.experimental import pallas as pl
from jax.experimental.pallas import tpu as pltpu
from jax.sharding import PartitionSpec as P

HEADS = 8
REACH = 6
EPS = 1e-05
FAR = -1e30
MESH = pl.DeviceIdType.MESH
F32 = jnp.float32
BF16 = jnp.bfloat16


def nn(a, b):
    return lax.dot_general(a, b, (((1,), (0,)), ((), ())), preferred_element_type=F32)


def nt(a, b):
    return lax.dot_general(a, b, (((1,), (1,)), ((), ())), preferred_element_type=F32)


def query_kernel(scale, lay, q_ref, g_ref, k_ref, v_ref, bias_ref, att_ref, gq_ref, stat_ref):
    h = pl.program_id(0)
    n_q = lay.own // 2

    @pl.when(h == 0)
    def _():
        stat_ref[...] = jnp.zeros(stat_ref.shape, F32)

    for half in range(2):
        out = slice(half * n_q, (half + 1) * n_q)
        rows = slice(lay.start + half * n_q, lay.start + (half + 1) * n_q)
        cols = lay.reach(half)
        k = k_ref[cols, :]
        v = v_ref[cols, :]
        s = nt(q_ref[rows, :], k) * scale + bias_ref[half]
        top = jnp.max(s, axis=-1, keepdims=True)
        e = jnp.exp(s - top)
        total = jnp.sum(e, axis=-1, keepdims=True)
        probs = e * (1.0 / total)
        att_ref[out, :] = nn(probs.astype(BF16), v).astype(BF16)
        gp = nt(g_ref[rows, :], v)
        spread = jnp.sum(probs * gp, axis=-1, keepdims=True)
        gs = (probs * (gp - spread) * scale).astype(BF16)
        gq_ref[out, :] = nn(gs, k).astype(BF16)
        lane = lax.broadcasted_iota(jnp.int32, (n_q, 128), 1)
        kept = jnp.where(lane == 2 * h + 1, spread, stat_ref[out, :])
        stat_ref[out, :] = jnp.where(lane == 2 * h, top + jnp.log(total), kept)


def key_kernel(scale, lay, k_ref, v_ref, q_ref, g_ref, bias_ref, stat_ref, gk_ref, gv_ref):
    h = pl.program_id(0)
    n_q = lay.own // 2
    for half in range(2):
        out = slice(half * n_q, (half + 1) * n_q)
        rows = slice(lay.start + half * n_q, lay.start + (half + 1) * n_q)
        cols = lay.reach(half)
        q = q_ref[cols, :]
        g = g_ref[cols, :]
        s = nt(k_ref[rows, :], q) * scale + bias_ref[half]
        probs = jnp.exp(s - stat_ref[half, pl.ds(2 * h, 1), :])
        gv_ref[out, :] = nn(probs.astype(BF16), g).astype(BF16)
        gp = nt(v_ref[rows, :], g)
        gs = (probs * (gp - stat_ref[half, pl.ds(2 * h + 1, 1), :]) * scale).astype(BF16)
        gk_ref[out, :] = nn(gs, q).astype(BF16)


def attention_calls(lay, width, model):
    scale = 1.0 / math.sqrt(width)
    own = pl.BlockSpec((lay.own, width), lambda h: (0, h))
    ext = pl.BlockSpec((lay.all, width), lambda h: (0, h))
    bias = pl.BlockSpec((2, lay.own // 2, lay.span), lambda h: (0, 0, 0))
    big = jax.ShapeDtypeStruct((lay.own, model), BF16)
    params = pltpu.CompilerParams(vmem_limit_bytes=32 * 1024 * 1024)
    first = pl.pallas_call(
        functools.partial(query_kernel, scale, lay),
        grid=(HEADS,),
        in_specs=[ext, ext, ext, ext, bias],
        out_specs=[own, own, pl.BlockSpec((lay.own, 128), lambda h: (0, 0))],
        out_shape=[big, big, jax.ShapeDtypeStruct((lay.own, 128), F32)],
        compiler_params=params,
    )
    second = pl.pallas_call(
        functools.partial(key_kernel, scale, lay),
        grid=(HEADS,),
        in_specs=[ext, ext, ext, ext, bias, pl.BlockSpec((2, 128, lay.span), lambda h: (0, 0, 0))],
        out_specs=[own, own],
        out_shape=[big, big],
        compiler_params=params,
    )
    return first, second


SIDES = ((0, 1), (0, -1), (1, 0), (-1, 0), (1, 1), (1, -1), (-1, 1), (-1, -1))


class Layout:
    def __init__(self, n_t, n_f):
        self.n_t, self.n_f = n_t, n_f
        self.own = n_t * n_f
        corner = -(-REACH * REACH // 16) * 16
        self.corner = corner
        sizes = {
            (-1, -1): corner,
            (-1, 1): corner,
            (-1, 0): REACH * n_f,
            (0, 0): self.own,
            (0, -1): REACH * n_t,
            (0, 1): REACH * n_t,
            (1, 0): REACH * n_f,
            (1, -1): corner,
            (1, 1): corner,
        }
        self.size = sizes
        self.at = {}
        self.all = 0
        for side, size in sizes.items():
            self.at[side] = self.all
            self.all += size
        self.start = self.at[0, 0]
        self.span = self.at[1, 0]

    def reach(self, half):
        return slice(0, self.span) if half == 0 else slice(self.start, self.all)

    def region(self, side):
        return slice(self.at[side], self.at[side] + self.size[side])

    def place(self, index):
        far = 1 << 20
        time = jnp.full(index.shape, far, jnp.int32)
        freq = jnp.full(index.shape, far, jnp.int32)
        for (dt, df), size in self.size.items():
            r = index - self.at[dt, df]
            n_col = self.n_f if df == 0 else REACH
            n_row = self.n_t if dt == 0 else REACH
            here = (r >= 0) & (r < n_row * n_col)
            t0 = 0 if dt == 0 else (-REACH if dt < 0 else self.n_t)
            f0 = 0 if df == 0 else (-REACH if df < 0 else self.n_f)
            time = jnp.where(here, t0 + r // n_col, time)
            freq = jnp.where(here, f0 + r % n_col, freq)
        return time, freq


def window_bias(lay):
    t0 = lax.axis_index("tm") * lay.n_t
    f0 = lax.axis_index("freq") * lay.n_f
    parts = []
    for half in range(2):
        own = half * (lay.own // 2) + jnp.arange(lay.own // 2)[:, None]
        cols = lay.reach(half)
        key_t, key_f = lay.place(jnp.arange(cols.start, cols.stop))
        inside = (
            (t0 + key_t >= 0)
            & (t0 + key_t < lay.n_t * lax.axis_size("tm"))
            & (f0 + key_f >= 0)
            & (f0 + key_f < lay.n_f * lax.axis_size("freq"))
        )
        ok = (
            (jnp.abs(key_t[None] - own // lay.n_f) <= REACH)
            & (jnp.abs(key_f[None] - own % lay.n_f) <= REACH)
            & inside[None]
        )
        parts.append(jnp.where(ok, 0.0, FAR).astype(F32))
    return jnp.stack(parts)


def opposite(side):
    return (-side[0], -side[1])


class Neighbours:
    def __init__(self):
        self.tm, self.fq = lax.axis_index("tm"), lax.axis_index("freq")
        self.t_size, self.f_size = lax.axis_size("tm"), lax.axis_size("freq")

    def exists(self, side):
        t, f = self.tm + side[0], self.fq + side[1]
        return (t >= 0) & (t < self.t_size) & (f >= 0) & (f < self.f_size)

    def device(self, side):
        return ((self.tm + side[0] + self.t_size) % self.t_size, (self.fq + side[1] + self.f_size) % self.f_size)

    def greet(self):
        barrier = pltpu.get_barrier_semaphore()
        for side in SIDES:

            @pl.when(self.exists(side))
            def _(side=side):
                pl.semaphore_signal(barrier, inc=1, device_id=self.device(side), device_id_type=MESH)

        pl.semaphore_wait(barrier, sum(self.exists(side).astype(jnp.int32) for side in SIDES))


class Exchange:
    def __init__(self, lay, near, source, send_sem, recv_sem):
        self.near, self.lay, self.nb = near, lay, Neighbours()
        self.source, self.send_sem, self.recv_sem = source, send_sem, recv_sem

    def copy(self, i):
        side = SIDES[i]
        to = self.lay.region(opposite(side))
        return pltpu.make_async_remote_copy(
            src_ref=self.source(side),
            dst_ref=self.near.at[pl.ds(to.start, to.stop - to.start)],
            send_sem=self.send_sem.at[i],
            recv_sem=self.recv_sem.at[i],
            device_id=self.nb.device(side),
            device_id_type=MESH,
        )

    def start(self):
        for i, side in enumerate(SIDES):

            @pl.when(self.nb.exists(side))
            def _(i=i):
                self.copy(i).start()

    def clear(self):
        for side in SIDES:

            @pl.when(jnp.logical_not(self.nb.exists(side)))
            def _(side=side):
                rows = self.lay.region(side)
                self.near[rows, :] = jnp.zeros((rows.stop - rows.start, self.near.shape[1]), self.near.dtype)

    def arrive(self):
        for i, side in enumerate(SIDES):

            @pl.when(self.nb.exists(opposite(side)))
            def _(i=i):
                self.copy(i).wait_recv()

    def sent(self):
        for i, side in enumerate(SIDES):

            @pl.when(self.nb.exists(side))
            def _(i=i):
                self.copy(i).wait_send()


def edge_source(lay, flat, sides, corners):
    n = REACH * lay.n_f

    def source(side):
        dt, df = side
        if df == 0:
            return flat.at[pl.ds(0 if dt < 0 else lay.own - n, n)]
        if dt == 0:
            return sides.at[0 if df < 0 else 1]
        return corners.at[(dt + 1) + (df + 1) // 2]

    return source


def project_kernel(lay, *refs):
    tok, tok_s, tok_c, grad, grad_s, grad_c, wq, wk, wv, wo = refs[:10]
    q_ref, k_ref, v_ref, g_ref, hid_ref = refs[10:15]
    near_tok, near_grad, hidden, wq_v, wk_v, wv_v, wo_v, w_sem, s_tok, r_tok, s_grad, r_grad = refs[15:]
    Neighbours().greet()
    toks = Exchange(lay, near_tok, edge_source(lay, tok, tok_s, tok_c), s_tok, r_tok)
    grads = Exchange(lay, near_grad, edge_source(lay, grad, grad_s, grad_c), s_grad, r_grad)
    toks.start()
    loads = [
        pltpu.make_async_copy(src, dst, w_sem.at[i])
        for i, (src, dst) in enumerate(((wq, wq_v), (wk, wk_v), (wv, wv_v), (wo, wo_v)))
    ]
    for load in loads:
        load.start()
    grads.start()
    toks.clear()
    grads.clear()

    def normalize(src, shift, start, stop):
        @pl.loop(0, (stop - start) // 32)
        def _(i):
            at = pl.multiple_of(start + i * 32, 32)
            wide = src[pl.ds(pl.multiple_of(at - shift, 32), 32), :].astype(F32)
            center = jnp.mean(wide, axis=-1, keepdims=True)
            shifted = wide - center
            inverse = lax.rsqrt(jnp.mean(shifted * shifted, axis=-1, keepdims=True) + EPS)
            hidden[pl.ds(at, 32), :] = (shifted * inverse).astype(BF16)

    a, b = lay.start, lay.start + lay.own
    normalize(tok, a, a, b)
    hid_ref[...] = hidden[a:b, :]
    for load in loads:
        load.wait()

    def rows(start, stop):
        for dst, w in ((q_ref, wq_v), (k_ref, wk_v), (v_ref, wv_v)):
            dst[start:stop, :] = nn(hidden[start:stop, :], w[...]).astype(BF16)

    rows(a, b)
    g_ref[a:b, :] = nt(grad[...], wo_v[...]).astype(BF16)
    toks.arrive()
    for start, stop in ((0, a), (b, lay.all)):
        normalize(near_tok, 0, start, stop)
        rows(start, stop)
    grads.arrive()
    for start, stop in ((0, a), (b, lay.all)):
        g_ref[start:stop, :] = nt(near_grad[start:stop, :], wo_v[...]).astype(BF16)
    toks.sent()
    grads.sent()


def strips(lay, m):
    n_t, n_f, model = m.shape
    sides = jnp.stack([m[:, :REACH], m[:, n_f - REACH :]]).reshape(2, REACH * n_t, model)
    corners = jnp.stack(
        [m[t, f].reshape(REACH * REACH, model) for t in (slice(0, REACH), slice(n_t - REACH, n_t))
         for f in (slice(0, REACH), slice(n_f - REACH, n_f))]
    )
    return sides, jnp.pad(corners, ((0, 0), (0, lay.corner - REACH * REACH), (0, 0)))


def project(lay, tokens, d_out, weights):
    model = tokens.shape[-1]
    vm, any_ = pl.BlockSpec(memory_space=pltpu.VMEM), pl.BlockSpec(memory_space=pl.ANY)
    ext = jax.ShapeDtypeStruct((lay.all, model), BF16)
    sem = pltpu.SemaphoreType.DMA((len(SIDES),))
    return pl.pallas_call(
        functools.partial(project_kernel, lay),
        out_shape=[ext] * 4 + [jax.ShapeDtypeStruct((lay.own, model), BF16)],
        in_specs=[vm] * 6 + [any_] * 4,
        out_specs=[vm] * 5,
        scratch_shapes=[pltpu.VMEM((lay.all, model), BF16)] * 3
        + [pltpu.VMEM(w.shape, BF16) for w in weights]
        + [pltpu.SemaphoreType.DMA((4,))]
        + [sem] * 4,
        compiler_params=pltpu.CompilerParams(
            collective_id=2, has_side_effects=True, vmem_limit_bytes=48 * 1024 * 1024
        ),
    )(
        tokens.reshape(lay.own, model),
        *strips(lay, tokens),
        d_out.reshape(lay.own, model),
        *strips(lay, d_out),
        *weights,
    )


def stats_kernel(lay, stat, att, tok, wo, near_ref, out_ref, near, sides, corners, s_sem, r_sem):
    n_t, n_f = lay.n_t, lay.n_f
    Neighbours().greet()
    corners[...] = jnp.zeros(corners.shape, F32)
    for t in range(n_t):
        sides[0, t * REACH : (t + 1) * REACH, :] = stat[t * n_f : t * n_f + REACH, :]
        sides[1, t * REACH : (t + 1) * REACH, :] = stat[(t + 1) * n_f - REACH : (t + 1) * n_f, :]
    for j, first in enumerate((0, n_t - REACH)):
        for r in range(REACH):
            at = (first + r) * n_f
            corners[2 * j, r * REACH : (r + 1) * REACH, :] = stat[at : at + REACH, :]
            corners[2 * j + 1, r * REACH : (r + 1) * REACH, :] = stat[at + n_f - REACH : at + n_f, :]
    ex = Exchange(lay, near, edge_source(lay, stat, sides, corners), s_sem, r_sem)
    ex.start()
    ex.clear()
    near[lay.region((0, 0)), :] = stat[...]
    out_ref[...] = (tok[...].astype(F32) + nn(att[...], wo[...])).astype(BF16)
    ex.arrive()
    for half in range(2):
        near_ref[half] = near[lay.reach(half), :].T
    ex.sent()


def exchange_stats(lay, stats, attended, flat, w_out):
    vm = pl.BlockSpec(memory_space=pltpu.VMEM)
    sem = pltpu.SemaphoreType.DMA((len(SIDES),))
    return pl.pallas_call(
        functools.partial(stats_kernel, lay),
        out_shape=[jax.ShapeDtypeStruct((2, 128, lay.span), F32), jax.ShapeDtypeStruct(flat.shape, BF16)],
        in_specs=[vm] * 4,
        out_specs=[vm] * 2,
        scratch_shapes=[
            pltpu.VMEM((lay.all, 128), F32),
            pltpu.VMEM((2, REACH * lay.n_t, 128), F32),
            pltpu.VMEM((4, lay.corner, 128), F32),
            sem,
            sem,
        ],
        compiler_params=pltpu.CompilerParams(
            collective_id=3, has_side_effects=True, vmem_limit_bytes=24 * 1024 * 1024
        ),
    )(stats, attended, flat, w_out)


def log2(n):
    return n.bit_length() - 1


def axis_orders(t_size, f_size):
    rest = [("freq", b) for b in range(log2(f_size))] + [("tm", b) for b in range(1, log2(t_size))]
    head, last = rest[:-1], rest[-1:]
    turns = [head[i:] + head[:i] for i in (2, 1, 0)] + [[head[1], head[0]] + head[2:]]
    return [[("tm", 0)] + turn + last for turn in turns]


def scatter_kernel(orders, sizes, *refs):
    n_mat = len(orders)
    n_st = len(orders[0])
    lefts = refs[:n_mat]
    rights = refs[n_mat : 2 * n_mat]
    out_ref = refs[2 * n_mat]
    total = refs[2 * n_mat + 1]
    sends = refs[2 * n_mat + 2 : 2 * n_mat + 2 + n_st]
    lands = refs[2 * n_mat + 2 + n_st : 2 * n_mat + 2 + 2 * n_st]
    send_sem, recv_sem = refs[-2:]
    tm, fq = lax.axis_index("tm"), lax.axis_index("freq")

    def bit(dim):
        axis, b = dim
        return ((tm if axis == "tm" else fq) // (1 << b)) % 2

    def partner(dim):
        axis, b = dim
        move = (1 - 2 * bit(dim)) * (1 << b)
        return (tm + move, fq) if axis == "tm" else (tm, fq + move)

    barrier = pltpu.get_barrier_semaphore()
    for dim in orders[0]:
        pl.semaphore_signal(barrier, inc=1, device_id=partner(dim), device_id_type=MESH)
    pl.semaphore_wait(barrier, n_st)

    def copy(m, st):
        return pltpu.make_async_remote_copy(
            src_ref=sends[st].at[m],
            dst_ref=lands[st].at[m],
            send_sem=send_sem.at[m, st],
            recv_sem=recv_sem.at[m, st],
            device_id=partner(orders[m][st]),
            device_id_type=MESH,
        )

    turn = list(range(n_mat - 1, -1, -1))
    half = sizes[0]
    for m in turn:
        theirs = pl.multiple_of((1 - bit(orders[m][0])) * half, half)
        sends[0][m] = nn(lefts[m][pl.ds(theirs, half), :], rights[m][...]).astype(BF16)
        copy(m, 0).start()
    for m in turn:
        mine = pl.multiple_of(bit(orders[m][0]) * half, half)
        total[m] = nn(lefts[m][pl.ds(mine, half), :], rights[m][...])
    base = [0] * n_mat
    for st in range(1, n_st):
        half = sizes[st]
        for m in turn:
            copy(m, st - 1).wait()
            b = bit(orders[m][st])
            theirs, mine = (1 - b) * half, b * half
            if half >= 16:
                theirs, mine = pl.multiple_of(theirs, half), pl.multiple_of(mine, half)
                there = pl.multiple_of(base[m] + theirs, half)
                here = pl.multiple_of(base[m] + mine, half)
                away = total[m, pl.ds(there, half), :] + lands[st - 1][m, pl.ds(theirs, half), :].astype(F32)
                sends[st][m] = away.astype(BF16)
                copy(m, st).start()
                total[m, pl.ds(here, half), :] += lands[st - 1][m, pl.ds(mine, half), :].astype(F32)
            else:
                start = pl.multiple_of(base[m], 2 * half)
                both = total[m, pl.ds(start, 2 * half), :] + lands[st - 1][m].astype(F32)
                low, high = both[:half], both[half:]
                away = jnp.where(b == 0, high, low)
                sends[st][m] = jnp.concatenate([away, away], axis=0).astype(BF16)
                copy(m, st).start()
                here = pl.multiple_of(base[m] + mine, half)
                total[m, pl.ds(here, half), :] = jnp.where(b == 0, low, high)
            base[m] = here
    half = sizes[-1]
    for m in turn:
        copy(m, n_st - 1).wait()
        out_ref[m] = total[m, pl.ds(base[m], half), :] + lands[-1][m].astype(F32)[0:half]


def scatter_sum(lefts, rights, t_size, f_size):
    n_dev = t_size * f_size
    n_st = log2(n_dev)
    orders = axis_orders(t_size, f_size)
    tokens, model = lefts[0].shape
    rows = model // n_dev
    sizes = [model >> (s + 1) for s in range(n_st)]
    flipped = []
    for left, order in zip(lefts, orders):
        place = [
            log2(t_size) - 1 - b if axis == "tm" else log2(t_size) + log2(f_size) - 1 - b for axis, b in order
        ]
        cube = left.T.reshape((2,) * n_st + (rows, tokens))
        flipped.append(cube.transpose(place + [n_st, n_st + 1]).reshape(model, tokens))
    n_mat = len(orders)
    blocks = [(n_mat, max(s, 16), model) for s in sizes]
    vm = pl.BlockSpec(memory_space=pltpu.VMEM)
    return pl.pallas_call(
        functools.partial(scatter_kernel, orders, sizes),
        out_shape=jax.ShapeDtypeStruct((n_mat, rows, model), F32),
        in_specs=[vm] * (2 * n_mat),
        out_specs=vm,
        scratch_shapes=[pltpu.VMEM((n_mat, sizes[0], model), F32)]
        + [pltpu.VMEM(b, BF16) for b in blocks]
        + [pltpu.VMEM(b, BF16) for b in blocks]
        + [pltpu.SemaphoreType.DMA((n_mat, n_st)), pltpu.SemaphoreType.DMA((n_mat, n_st))],
        compiler_params=pltpu.CompilerParams(
            collective_id=1, has_side_effects=True, vmem_limit_bytes=56 * 1024 * 1024
        ),
        cost_estimate=pl.CostEstimate(
            flops=2 * n_mat * tokens * model * model, bytes_accessed=4 * tokens * model, transcendentals=0
        ),
    )(*flipped, *rights)


def layer_norm(flat_rows):
    wide = flat_rows.astype(F32)
    center = jnp.mean(wide, axis=-1, keepdims=True)
    shifted = wide - center
    inverse = lax.rsqrt(jnp.mean(shifted * shifted, axis=-1, keepdims=True) + EPS)
    return shifted * inverse, inverse


def local(tokens, w_query, w_key, w_value, w_out, d_out):
    n_t, n_f, model = tokens.shape
    lay = Layout(n_t, n_f)
    flat = tokens.reshape(lay.own, model)
    grad_flat = d_out.reshape(lay.own, model)
    normed, inverse = layer_norm(flat)
    bias = window_bias(lay)
    query, key, value, grad_att, hidden = project(lay, tokens, d_out, (w_query, w_key, w_value, w_out))
    first, second = attention_calls(lay, model // HEADS, model)
    attended, grad_query, stats = first(query, grad_att, key, value, bias)
    near_stats, output = exchange_stats(lay, stats, attended, flat, w_out)
    grad_key, grad_value = second(key, value, query, grad_att, bias, near_stats)

    weight_grads = scatter_sum(
        [hidden, hidden, hidden, attended],
        [grad_query, grad_key, grad_value, grad_flat],
        lax.axis_size("tm"),
        lax.axis_size("freq"),
    ).transpose(1, 0, 2)

    grad_hidden = nt(grad_query, w_query) + nt(grad_key, w_key) + nt(grad_value, w_value)
    center = jnp.mean(grad_hidden, axis=-1, keepdims=True)
    along = jnp.mean(grad_hidden * normed, axis=-1, keepdims=True)
    input_grad = (grad_flat.astype(F32) + (grad_hidden - center - normed * along) * inverse).astype(BF16)
    return output.reshape(n_t, n_f, model), input_grad.reshape(n_t, n_f, model), weight_grads


def solution(mesh):
    tile = P("tm", "freq", None)
    in_specs = (tile, P(), P(), P(), P(), tile)
    out_specs = (tile, tile, P(("tm", "freq"), None, None))
    return jax.shard_map(local, mesh=mesh, in_specs=in_specs, out_specs=out_specs, check_vma=False)
```

```python
import functools
import math

import jax
import jax.numpy as jnp
from jax import lax
from jax.experimental import pallas as pl
from jax.experimental.pallas import tpu as pltpu
from jax.sharding import PartitionSpec as P

HEADS = 8
REACH = 6
EPS = 1e-05
FAR = -1e30
MESH = pl.DeviceIdType.MESH
F32 = jnp.float32
BF16 = jnp.bfloat16


def nn(a, b):
    return lax.dot_general(a, b, (((1,), (0,)), ((), ())), preferred_element_type=F32)


def nt(a, b):
    return lax.dot_general(a, b, (((1,), (1,)), ((), ())), preferred_element_type=F32)


def query_kernel(scale, lay, *refs):
    q_ref, g_ref, k_ref, v_ref, bias_ref, grad, grad_s, grad_c = refs[:8]
    att_ref, gq_ref, stat_ref, far_ref, near, s_sem, r_sem = refs[8:]
    h = pl.program_id(0)
    n_q = lay.own // 2
    ex = Exchange(lay, near, edge_source(lay, grad, grad_s, grad_c), s_sem, r_sem)

    @pl.when(h == 0)
    def _():
        ex.nb.greet()
        ex.start()
        ex.clear()
        stat_ref[...] = jnp.zeros(stat_ref.shape, F32)

    for half in range(2):
        out = slice(half * n_q, (half + 1) * n_q)
        rows = slice(lay.start + half * n_q, lay.start + (half + 1) * n_q)
        cols = lay.reach(half)
        k = k_ref[cols, :]
        v = v_ref[cols, :]
        s = nt(q_ref[rows, :], k) * scale + bias_ref[half]
        top = jnp.max(s, axis=-1, keepdims=True)
        e = jnp.exp(s - top)
        total = jnp.sum(e, axis=-1, keepdims=True)
        probs = e * (1.0 / total)
        att_ref[out, :] = nn(probs.astype(BF16), v).astype(BF16)
        gp = nt(g_ref[out, :], v)
        spread = jnp.sum(probs * gp, axis=-1, keepdims=True)
        gs = (probs * (gp - spread) * scale).astype(BF16)
        gq_ref[out, :] = nn(gs, k).astype(BF16)
        lane = lax.broadcasted_iota(jnp.int32, (n_q, 128), 1)
        kept = jnp.where(lane == 2 * h + 1, spread, stat_ref[out, :])
        stat_ref[out, :] = jnp.where(lane == 2 * h, top + jnp.log(total), kept)

    @pl.when(h == HEADS - 1)
    def _():
        ex.arrive()
        far_ref[: lay.start, :] = near[: lay.start, :]
        far_ref[lay.start : lay.start + lay.own, :] = jnp.zeros((lay.own, near.shape[1]), BF16)
        far_ref[lay.start + lay.own :, :] = near[lay.start + lay.own :, :]
        ex.sent()


def key_kernel(scale, lay, k_ref, v_ref, q_ref, g_ref, bias_ref, stat_ref, gk_ref, gv_ref):
    h = pl.program_id(0)
    n_q = lay.own // 2
    for half in range(2):
        out = slice(half * n_q, (half + 1) * n_q)
        rows = slice(lay.start + half * n_q, lay.start + (half + 1) * n_q)
        cols = lay.reach(half)
        q = q_ref[cols, :]
        g = g_ref[cols, :]
        s = nt(k_ref[rows, :], q) * scale + bias_ref[half]
        probs = jnp.exp(s - stat_ref[half, pl.ds(2 * h, 1), :])
        gv_ref[out, :] = nn(probs.astype(BF16), g).astype(BF16)
        gp = nt(v_ref[rows, :], g)
        gs = (probs * (gp - stat_ref[half, pl.ds(2 * h + 1, 1), :]) * scale).astype(BF16)
        gk_ref[out, :] = nn(gs, q).astype(BF16)


def attention_calls(lay, width, model):
    scale = 1.0 / math.sqrt(width)
    own = pl.BlockSpec((lay.own, width), lambda h: (0, h))
    ext = pl.BlockSpec((lay.all, width), lambda h: (0, h))
    bias = pl.BlockSpec((2, lay.own // 2, lay.span), lambda h: (0, 0, 0))
    big = jax.ShapeDtypeStruct((lay.own, model), BF16)
    params = pltpu.CompilerParams(vmem_limit_bytes=32 * 1024 * 1024)
    first = pl.pallas_call(
        functools.partial(query_kernel, scale, lay),
        grid=(HEADS,),
        in_specs=[ext, own, ext, ext, bias] + [pl.BlockSpec(memory_space=pl.ANY)] * 3,
        out_specs=[
            own,
            own,
            pl.BlockSpec((lay.own, 128), lambda h: (0, 0)),
            pl.BlockSpec((lay.all, model), lambda h: (0, 0)),
        ],
        out_shape=[
            big,
            big,
            jax.ShapeDtypeStruct((lay.own, 128), F32),
            jax.ShapeDtypeStruct((lay.all, model), BF16),
        ],
        scratch_shapes=[pltpu.VMEM((lay.all, model), BF16)] + [pltpu.SemaphoreType.DMA((len(SIDES),))] * 2,
        compiler_params=pltpu.CompilerParams(
            collective_id=4, has_side_effects=True, vmem_limit_bytes=32 * 1024 * 1024
        ),
    )
    second = pl.pallas_call(
        functools.partial(key_kernel, scale, lay),
        grid=(HEADS,),
        in_specs=[ext, ext, ext, ext, bias, pl.BlockSpec((2, 128, lay.span), lambda h: (0, 0, 0))],
        out_specs=[own, own],
        out_shape=[big, big],
        compiler_params=params,
    )
    return first, second


SIDES = ((0, 1), (0, -1), (1, 0), (-1, 0), (1, 1), (1, -1), (-1, 1), (-1, -1))


class Layout:
    def __init__(self, n_t, n_f):
        self.n_t, self.n_f = n_t, n_f
        self.own = n_t * n_f
        corner = -(-REACH * REACH // 16) * 16
        self.corner = corner
        sizes = {
            (-1, -1): corner,
            (-1, 1): corner,
            (-1, 0): REACH * n_f,
            (0, 0): self.own,
            (0, -1): REACH * n_t,
            (0, 1): REACH * n_t,
            (1, 0): REACH * n_f,
            (1, -1): corner,
            (1, 1): corner,
        }
        self.size = sizes
        self.at = {}
        self.all = 0
        for side, size in sizes.items():
            self.at[side] = self.all
            self.all += size
        self.start = self.at[0, 0]
        self.span = self.at[1, 0]

    def reach(self, half):
        return slice(0, self.span) if half == 0 else slice(self.start, self.all)

    def region(self, side):
        return slice(self.at[side], self.at[side] + self.size[side])

    def place(self, index):
        far = 1 << 20
        time = jnp.full(index.shape, far, jnp.int32)
        freq = jnp.full(index.shape, far, jnp.int32)
        for (dt, df), size in self.size.items():
            r = index - self.at[dt, df]
            n_col = self.n_f if df == 0 else REACH
            n_row = self.n_t if dt == 0 else REACH
            here = (r >= 0) & (r < n_row * n_col)
            t0 = 0 if dt == 0 else (-REACH if dt < 0 else self.n_t)
            f0 = 0 if df == 0 else (-REACH if df < 0 else self.n_f)
            time = jnp.where(here, t0 + r // n_col, time)
            freq = jnp.where(here, f0 + r % n_col, freq)
        return time, freq


def window_bias(lay):
    t0 = lax.axis_index("tm") * lay.n_t
    f0 = lax.axis_index("freq") * lay.n_f
    parts = []
    for half in range(2):
        own = half * (lay.own // 2) + jnp.arange(lay.own // 2)[:, None]
        cols = lay.reach(half)
        key_t, key_f = lay.place(jnp.arange(cols.start, cols.stop))
        inside = (
            (t0 + key_t >= 0)
            & (t0 + key_t < lay.n_t * lax.axis_size("tm"))
            & (f0 + key_f >= 0)
            & (f0 + key_f < lay.n_f * lax.axis_size("freq"))
        )
        ok = (
            (jnp.abs(key_t[None] - own // lay.n_f) <= REACH)
            & (jnp.abs(key_f[None] - own % lay.n_f) <= REACH)
            & inside[None]
        )
        parts.append(jnp.where(ok, 0.0, FAR).astype(F32))
    return jnp.stack(parts)


def opposite(side):
    return (-side[0], -side[1])


class Neighbours:
    def __init__(self):
        self.tm, self.fq = lax.axis_index("tm"), lax.axis_index("freq")
        self.t_size, self.f_size = lax.axis_size("tm"), lax.axis_size("freq")

    def exists(self, side):
        t, f = self.tm + side[0], self.fq + side[1]
        return (t >= 0) & (t < self.t_size) & (f >= 0) & (f < self.f_size)

    def device(self, side):
        return ((self.tm + side[0] + self.t_size) % self.t_size, (self.fq + side[1] + self.f_size) % self.f_size)

    def greet(self):
        barrier = pltpu.get_barrier_semaphore()
        for side in SIDES:

            @pl.when(self.exists(side))
            def _(side=side):
                pl.semaphore_signal(barrier, inc=1, device_id=self.device(side), device_id_type=MESH)

        pl.semaphore_wait(barrier, sum(self.exists(side).astype(jnp.int32) for side in SIDES))


class Exchange:
    def __init__(self, lay, near, source, send_sem, recv_sem):
        self.near, self.lay, self.nb = near, lay, Neighbours()
        self.source, self.send_sem, self.recv_sem = source, send_sem, recv_sem

    def copy(self, i):
        side = SIDES[i]
        to = self.lay.region(opposite(side))
        return pltpu.make_async_remote_copy(
            src_ref=self.source(side),
            dst_ref=self.near.at[pl.ds(to.start, to.stop - to.start)],
            send_sem=self.send_sem.at[i],
            recv_sem=self.recv_sem.at[i],
            device_id=self.nb.device(side),
            device_id_type=MESH,
        )

    def start(self):
        for i, side in enumerate(SIDES):

            @pl.when(self.nb.exists(side))
            def _(i=i):
                self.copy(i).start()

    def clear(self):
        for side in SIDES:

            @pl.when(jnp.logical_not(self.nb.exists(side)))
            def _(side=side):
                rows = self.lay.region(side)
                self.near[rows, :] = jnp.zeros((rows.stop - rows.start, self.near.shape[1]), self.near.dtype)

    def arrive(self):
        for i, side in enumerate(SIDES):

            @pl.when(self.nb.exists(opposite(side)))
            def _(i=i):
                self.copy(i).wait_recv()

    def sent(self):
        for i, side in enumerate(SIDES):

            @pl.when(self.nb.exists(side))
            def _(i=i):
                self.copy(i).wait_send()


def edge_source(lay, flat, sides, corners):
    n = REACH * lay.n_f

    def source(side):
        dt, df = side
        if df == 0:
            return flat.at[pl.ds(0 if dt < 0 else lay.own - n, n)]
        if dt == 0:
            return sides.at[0 if df < 0 else 1]
        return corners.at[(dt + 1) + (df + 1) // 2]

    return source


def project_kernel(lay, *refs):
    tok, tok_s, tok_c, grad, wq, wk, wv, wo = refs[:8]
    q_ref, k_ref, v_ref, g_ref, hid_ref = refs[8:13]
    near_tok, hidden, wq_v, wk_v, wv_v, wo_v, w_sem, s_tok, r_tok = refs[13:]
    Neighbours().greet()
    toks = Exchange(lay, near_tok, edge_source(lay, tok, tok_s, tok_c), s_tok, r_tok)
    toks.start()
    loads = [
        pltpu.make_async_copy(src, dst, w_sem.at[i])
        for i, (src, dst) in enumerate(((wq, wq_v), (wk, wk_v), (wv, wv_v), (wo, wo_v)))
    ]
    for load in loads:
        load.start()
    toks.clear()

    def normalize(src, shift, start, stop):
        @pl.loop(0, (stop - start) // 32)
        def _(i):
            at = pl.multiple_of(start + i * 32, 32)
            wide = src[pl.ds(pl.multiple_of(at - shift, 32), 32), :].astype(F32)
            center = jnp.mean(wide, axis=-1, keepdims=True)
            shifted = wide - center
            inverse = lax.rsqrt(jnp.mean(shifted * shifted, axis=-1, keepdims=True) + EPS)
            hidden[pl.ds(at, 32), :] = (shifted * inverse).astype(BF16)

    a, b = lay.start, lay.start + lay.own
    normalize(tok, a, a, b)
    hid_ref[...] = hidden[a:b, :]
    for load in loads:
        load.wait()

    def rows(start, stop):
        for dst, w in ((q_ref, wq_v), (k_ref, wk_v), (v_ref, wv_v)):
            dst[start:stop, :] = nn(hidden[start:stop, :], w[...]).astype(BF16)

    rows(a, b)
    g_ref[...] = nt(grad[...], wo_v[...]).astype(BF16)
    toks.arrive()
    for start, stop in ((0, a), (b, lay.all)):
        normalize(near_tok, 0, start, stop)
        rows(start, stop)
    toks.sent()


def strips(lay, m):
    n_t, n_f, model = m.shape
    sides = jnp.stack([m[:, :REACH], m[:, n_f - REACH :]]).reshape(2, REACH * n_t, model)
    corners = jnp.stack(
        [m[t, f].reshape(REACH * REACH, model) for t in (slice(0, REACH), slice(n_t - REACH, n_t))
         for f in (slice(0, REACH), slice(n_f - REACH, n_f))]
    )
    return sides, jnp.pad(corners, ((0, 0), (0, lay.corner - REACH * REACH), (0, 0)))


def project(lay, tokens, d_out, weights):
    model = tokens.shape[-1]
    vm, any_ = pl.BlockSpec(memory_space=pltpu.VMEM), pl.BlockSpec(memory_space=pl.ANY)
    ext = jax.ShapeDtypeStruct((lay.all, model), BF16)
    sem = pltpu.SemaphoreType.DMA((len(SIDES),))
    return pl.pallas_call(
        functools.partial(project_kernel, lay),
        out_shape=[ext] * 3 + [jax.ShapeDtypeStruct((lay.own, model), BF16)] * 2,
        in_specs=[vm] * 4 + [any_] * 4,
        out_specs=[vm] * 5,
        scratch_shapes=[pltpu.VMEM((lay.all, model), BF16)] * 2
        + [pltpu.VMEM(w.shape, BF16) for w in weights]
        + [pltpu.SemaphoreType.DMA((4,))]
        + [sem] * 2,
        compiler_params=pltpu.CompilerParams(
            collective_id=2, has_side_effects=True, vmem_limit_bytes=48 * 1024 * 1024
        ),
    )(
        tokens.reshape(lay.own, model),
        *strips(lay, tokens),
        d_out.reshape(lay.own, model),
        *weights,
    )


def stats_kernel(lay, stat, att, tok, wo, own_g, far, near_ref, out_ref, g_ref, near, sides, corners, s_sem, r_sem):
    n_t, n_f = lay.n_t, lay.n_f
    Neighbours().greet()
    corners[...] = jnp.zeros(corners.shape, F32)
    for t in range(n_t):
        sides[0, t * REACH : (t + 1) * REACH, :] = stat[t * n_f : t * n_f + REACH, :]
        sides[1, t * REACH : (t + 1) * REACH, :] = stat[(t + 1) * n_f - REACH : (t + 1) * n_f, :]
    for j, first in enumerate((0, n_t - REACH)):
        for r in range(REACH):
            at = (first + r) * n_f
            corners[2 * j, r * REACH : (r + 1) * REACH, :] = stat[at : at + REACH, :]
            corners[2 * j + 1, r * REACH : (r + 1) * REACH, :] = stat[at + n_f - REACH : at + n_f, :]
    ex = Exchange(lay, near, edge_source(lay, stat, sides, corners), s_sem, r_sem)
    ex.start()
    ex.clear()
    near[lay.region((0, 0)), :] = stat[...]
    out_ref[...] = (tok[...].astype(F32) + nn(att[...], wo[...])).astype(BF16)
    a, b = lay.start, lay.start + lay.own
    g_ref[:a, :] = nt(far[:a, :], wo[...]).astype(BF16)
    g_ref[a:b, :] = own_g[...]
    g_ref[b:, :] = nt(far[b:, :], wo[...]).astype(BF16)
    ex.arrive()
    for half in range(2):
        near_ref[half] = near[lay.reach(half), :].T
    ex.sent()


def exchange_stats(lay, stats, attended, flat, w_out, grad_att, far):
    vm = pl.BlockSpec(memory_space=pltpu.VMEM)
    sem = pltpu.SemaphoreType.DMA((len(SIDES),))
    return pl.pallas_call(
        functools.partial(stats_kernel, lay),
        out_shape=[
            jax.ShapeDtypeStruct((2, 128, lay.span), F32),
            jax.ShapeDtypeStruct(flat.shape, BF16),
            jax.ShapeDtypeStruct(far.shape, BF16),
        ],
        in_specs=[vm] * 6,
        out_specs=[vm] * 3,
        scratch_shapes=[
            pltpu.VMEM((lay.all, 128), F32),
            pltpu.VMEM((2, REACH * lay.n_t, 128), F32),
            pltpu.VMEM((4, lay.corner, 128), F32),
            sem,
            sem,
        ],
        compiler_params=pltpu.CompilerParams(
            collective_id=3, has_side_effects=True, vmem_limit_bytes=24 * 1024 * 1024
        ),
    )(stats, attended, flat, w_out, grad_att, far)


def log2(n):
    return n.bit_length() - 1


def axis_orders(t_size, f_size):
    rest = [("freq", b) for b in range(log2(f_size))] + [("tm", b) for b in range(1, log2(t_size))]
    head, last = rest[:-1], rest[-1:]
    turns = [head[i:] + head[:i] for i in (2, 1, 0)] + [[head[1], head[0]] + head[2:]]
    return [[("tm", 0)] + turn + last for turn in turns]


def scatter_kernel(orders, sizes, *refs):
    n_mat = len(orders)
    n_st = len(orders[0])
    lefts = refs[:n_mat]
    rights = refs[n_mat : 2 * n_mat]
    out_ref = refs[2 * n_mat]
    total = refs[2 * n_mat + 1]
    sends = refs[2 * n_mat + 2 : 2 * n_mat + 2 + n_st]
    lands = refs[2 * n_mat + 2 + n_st : 2 * n_mat + 2 + 2 * n_st]
    send_sem, recv_sem = refs[-2:]
    tm, fq = lax.axis_index("tm"), lax.axis_index("freq")

    def bit(dim):
        axis, b = dim
        return ((tm if axis == "tm" else fq) // (1 << b)) % 2

    def partner(dim):
        axis, b = dim
        move = (1 - 2 * bit(dim)) * (1 << b)
        return (tm + move, fq) if axis == "tm" else (tm, fq + move)

    barrier = pltpu.get_barrier_semaphore()
    for dim in orders[0]:
        pl.semaphore_signal(barrier, inc=1, device_id=partner(dim), device_id_type=MESH)
    pl.semaphore_wait(barrier, n_st)

    def copy(m, st):
        return pltpu.make_async_remote_copy(
            src_ref=sends[st].at[m],
            dst_ref=lands[st].at[m],
            send_sem=send_sem.at[m, st],
            recv_sem=recv_sem.at[m, st],
            device_id=partner(orders[m][st]),
            device_id_type=MESH,
        )

    turn = list(range(n_mat - 1, -1, -1))
    half = sizes[0]
    for m in turn:
        theirs = pl.multiple_of((1 - bit(orders[m][0])) * half, half)
        sends[0][m] = nn(lefts[m][pl.ds(theirs, half), :], rights[m][...]).astype(BF16)
        copy(m, 0).start()
    for m in turn:
        mine = pl.multiple_of(bit(orders[m][0]) * half, half)
        total[m] = nn(lefts[m][pl.ds(mine, half), :], rights[m][...])
    base = [0] * n_mat
    for st in range(1, n_st):
        half = sizes[st]
        for m in turn:
            copy(m, st - 1).wait()
            b = bit(orders[m][st])
            theirs, mine = (1 - b) * half, b * half
            if half >= 16:
                theirs, mine = pl.multiple_of(theirs, half), pl.multiple_of(mine, half)
                there = pl.multiple_of(base[m] + theirs, half)
                here = pl.multiple_of(base[m] + mine, half)
                away = total[m, pl.ds(there, half), :] + lands[st - 1][m, pl.ds(theirs, half), :].astype(F32)
                sends[st][m] = away.astype(BF16)
                copy(m, st).start()
                total[m, pl.ds(here, half), :] += lands[st - 1][m, pl.ds(mine, half), :].astype(F32)
            else:
                start = pl.multiple_of(base[m], 2 * half)
                both = total[m, pl.ds(start, 2 * half), :] + lands[st - 1][m].astype(F32)
                low, high = both[:half], both[half:]
                away = jnp.where(b == 0, high, low)
                sends[st][m] = jnp.concatenate([away, away], axis=0).astype(BF16)
                copy(m, st).start()
                here = pl.multiple_of(base[m] + mine, half)
                total[m, pl.ds(here, half), :] = jnp.where(b == 0, low, high)
            base[m] = here
    half = sizes[-1]
    for m in turn:
        copy(m, n_st - 1).wait()
        out_ref[m] = total[m, pl.ds(base[m], half), :] + lands[-1][m].astype(F32)[0:half]


def scatter_sum(lefts, rights, t_size, f_size):
    n_dev = t_size * f_size
    n_st = log2(n_dev)
    orders = axis_orders(t_size, f_size)
    tokens, model = lefts[0].shape
    rows = model // n_dev
    sizes = [model >> (s + 1) for s in range(n_st)]
    flipped = []
    for left, order in zip(lefts, orders):
        place = [
            log2(t_size) - 1 - b if axis == "tm" else log2(t_size) + log2(f_size) - 1 - b for axis, b in order
        ]
        cube = left.T.reshape((2,) * n_st + (rows, tokens))
        flipped.append(cube.transpose(place + [n_st, n_st + 1]).reshape(model, tokens))
    n_mat = len(orders)
    blocks = [(n_mat, max(s, 16), model) for s in sizes]
    vm = pl.BlockSpec(memory_space=pltpu.VMEM)
    return pl.pallas_call(
        functools.partial(scatter_kernel, orders, sizes),
        out_shape=jax.ShapeDtypeStruct((n_mat, rows, model), F32),
        in_specs=[vm] * (2 * n_mat),
        out_specs=vm,
        scratch_shapes=[pltpu.VMEM((n_mat, sizes[0], model), F32)]
        + [pltpu.VMEM(b, BF16) for b in blocks]
        + [pltpu.VMEM(b, BF16) for b in blocks]
        + [pltpu.SemaphoreType.DMA((n_mat, n_st)), pltpu.SemaphoreType.DMA((n_mat, n_st))],
        compiler_params=pltpu.CompilerParams(
            collective_id=1, has_side_effects=True, vmem_limit_bytes=56 * 1024 * 1024
        ),
        cost_estimate=pl.CostEstimate(
            flops=2 * n_mat * tokens * model * model, bytes_accessed=4 * tokens * model, transcendentals=0
        ),
    )(*flipped, *rights)


def layer_norm(flat_rows):
    wide = flat_rows.astype(F32)
    center = jnp.mean(wide, axis=-1, keepdims=True)
    shifted = wide - center
    inverse = lax.rsqrt(jnp.mean(shifted * shifted, axis=-1, keepdims=True) + EPS)
    return shifted * inverse, inverse


def local(tokens, w_query, w_key, w_value, w_out, d_out):
    n_t, n_f, model = tokens.shape
    lay = Layout(n_t, n_f)
    flat = tokens.reshape(lay.own, model)
    grad_flat = d_out.reshape(lay.own, model)
    normed, inverse = layer_norm(flat)
    bias = window_bias(lay)
    query, key, value, grad_att, hidden = project(lay, tokens, d_out, (w_query, w_key, w_value, w_out))
    first, second = attention_calls(lay, model // HEADS, model)
    attended, grad_query, stats, far = first(query, grad_att, key, value, bias, grad_flat, *strips(lay, d_out))
    near_stats, output, near_gatt = exchange_stats(lay, stats, attended, flat, w_out, grad_att, far)
    grad_key, grad_value = second(key, value, query, near_gatt, bias, near_stats)

    weight_grads = scatter_sum(
        [hidden, hidden, hidden, attended],
        [grad_query, grad_key, grad_value, grad_flat],
        lax.axis_size("tm"),
        lax.axis_size("freq"),
    ).transpose(1, 0, 2)

    grad_hidden = nt(grad_query, w_query) + nt(grad_key, w_key) + nt(grad_value, w_value)
    center = jnp.mean(grad_hidden, axis=-1, keepdims=True)
    along = jnp.mean(grad_hidden * normed, axis=-1, keepdims=True)
    input_grad = (grad_flat.astype(F32) + (grad_hidden - center - normed * along) * inverse).astype(BF16)
    return output.reshape(n_t, n_f, model), input_grad.reshape(n_t, n_f, model), weight_grads


def solution(mesh):
    tile = P("tm", "freq", None)
    in_specs = (tile, P(), P(), P(), P(), tile)
    out_specs = (tile, tile, P(("tm", "freq"), None, None))
    return jax.shard_map(local, mesh=mesh, in_specs=in_specs, out_specs=out_specs, check_vma=False)
```

```python
import functools
import math

import jax
import jax.numpy as jnp
from jax import lax
from jax.experimental import pallas as pl
from jax.experimental.pallas import tpu as pltpu
from jax.sharding import PartitionSpec as P

HEADS = 8
REACH = 6
EPS = 1e-05
FAR = -1e30
MESH = pl.DeviceIdType.MESH
F32 = jnp.float32
BF16 = jnp.bfloat16


def nn(a, b):
    return lax.dot_general(a, b, (((1,), (0,)), ((), ())), preferred_element_type=F32)


def nt(a, b):
    return lax.dot_general(a, b, (((1,), (1,)), ((), ())), preferred_element_type=F32)


def query_kernel(scale, lay, *refs):
    q_ref, g_ref, k_ref, v_ref, bias_ref, grad, grad_s, grad_c = refs[:8]
    att_ref, gq_ref, stat_ref, far_ref, near, s_sem, r_sem = refs[8:]
    h = pl.program_id(0)
    n_q = lay.own // 2
    ex = Exchange(lay, near, edge_source(lay, grad, grad_s, grad_c), s_sem, r_sem)

    @pl.when(h == 0)
    def _():
        ex.nb.greet()
        ex.start()
        ex.clear()
        stat_ref[...] = jnp.zeros(stat_ref.shape, F32)

    for half in range(2):
        out = slice(half * n_q, (half + 1) * n_q)
        rows = slice(lay.start + half * n_q, lay.start + (half + 1) * n_q)
        cols = lay.reach(half)
        k = k_ref[cols, :]
        v = v_ref[cols, :]
        s = nt(q_ref[rows, :], k) * scale + bias_ref[half]
        top = jnp.max(s, axis=-1, keepdims=True)
        e = jnp.exp(s - top)
        total = jnp.sum(e, axis=-1, keepdims=True)
        probs = e * (1.0 / total)
        att_ref[out, :] = nn(probs.astype(BF16), v).astype(BF16)
        gp = nt(g_ref[out, :], v)
        spread = jnp.sum(probs * gp, axis=-1, keepdims=True)
        gs = (probs * (gp - spread) * scale).astype(BF16)
        gq_ref[out, :] = nn(gs, k).astype(BF16)
        lane = lax.broadcasted_iota(jnp.int32, (n_q, 128), 1)
        kept = jnp.where(lane == 2 * h + 1, spread, stat_ref[out, :])
        stat_ref[out, :] = jnp.where(lane == 2 * h, top + jnp.log(total), kept)

    @pl.when(h == HEADS - 1)
    def _():
        ex.arrive()
        far_ref[: lay.start, :] = near[: lay.start, :]
        far_ref[lay.start : lay.start + lay.own, :] = jnp.zeros((lay.own, near.shape[1]), BF16)
        far_ref[lay.start + lay.own :, :] = near[lay.start + lay.own :, :]
        ex.sent()


def key_pass(scale, lay, width, k_ref, v_ref, q_ref, g_ref, bias_ref, stat_ref, gk_ref, gv_ref):
    n_q = lay.own // 2

    @pl.loop(0, HEADS)
    def _(h):
        lanes = pl.ds(pl.multiple_of(h * width, width), width)
        for half in range(2):
            out = slice(half * n_q, (half + 1) * n_q)
            rows = slice(lay.start + half * n_q, lay.start + (half + 1) * n_q)
            cols = lay.reach(half)
            q = q_ref[cols, lanes]
            g = g_ref[cols, lanes]
            s = nt(k_ref[rows, lanes], q) * scale + bias_ref[half]
            probs = jnp.exp(s - stat_ref[half, pl.ds(2 * h, 1), :])
            gv_ref[out, lanes] = nn(probs.astype(BF16), g).astype(BF16)
            gp = nt(v_ref[rows, lanes], g)
            gs = (probs * (gp - stat_ref[half, pl.ds(2 * h + 1, 1), :]) * scale).astype(BF16)
            gk_ref[out, lanes] = nn(gs, q).astype(BF16)


def attention_calls(lay, width, model):
    scale = 1.0 / math.sqrt(width)
    own = pl.BlockSpec((lay.own, width), lambda h: (0, h))
    ext = pl.BlockSpec((lay.all, width), lambda h: (0, h))
    bias = pl.BlockSpec((2, lay.own // 2, lay.span), lambda h: (0, 0, 0))
    big = jax.ShapeDtypeStruct((lay.own, model), BF16)
    params = pltpu.CompilerParams(vmem_limit_bytes=32 * 1024 * 1024)
    first = pl.pallas_call(
        functools.partial(query_kernel, scale, lay),
        grid=(HEADS,),
        in_specs=[ext, own, ext, ext, bias] + [pl.BlockSpec(memory_space=pl.ANY)] * 3,
        out_specs=[
            own,
            own,
            pl.BlockSpec((lay.own, 128), lambda h: (0, 0)),
            pl.BlockSpec((lay.all, model), lambda h: (0, 0)),
        ],
        out_shape=[
            big,
            big,
            jax.ShapeDtypeStruct((lay.own, 128), F32),
            jax.ShapeDtypeStruct((lay.all, model), BF16),
        ],
        scratch_shapes=[pltpu.VMEM((lay.all, model), BF16)] + [pltpu.SemaphoreType.DMA((len(SIDES),))] * 2,
        compiler_params=pltpu.CompilerParams(
            collective_id=4, has_side_effects=True, vmem_limit_bytes=32 * 1024 * 1024
        ),
    )
    return first


SIDES = ((0, 1), (0, -1), (1, 0), (-1, 0), (1, 1), (1, -1), (-1, 1), (-1, -1))


class Layout:
    def __init__(self, n_t, n_f):
        self.n_t, self.n_f = n_t, n_f
        self.own = n_t * n_f
        corner = -(-REACH * REACH // 16) * 16
        self.corner = corner
        sizes = {
            (-1, -1): corner,
            (-1, 1): corner,
            (-1, 0): REACH * n_f,
            (0, 0): self.own,
            (0, -1): REACH * n_t,
            (0, 1): REACH * n_t,
            (1, 0): REACH * n_f,
            (1, -1): corner,
            (1, 1): corner,
        }
        self.size = sizes
        self.at = {}
        self.all = 0
        for side, size in sizes.items():
            self.at[side] = self.all
            self.all += size
        self.start = self.at[0, 0]
        self.span = self.at[1, 0]

    def reach(self, half):
        return slice(0, self.span) if half == 0 else slice(self.start, self.all)

    def region(self, side):
        return slice(self.at[side], self.at[side] + self.size[side])

    def place(self, index):
        far = 1 << 20
        time = jnp.full(index.shape, far, jnp.int32)
        freq = jnp.full(index.shape, far, jnp.int32)
        for (dt, df), size in self.size.items():
            r = index - self.at[dt, df]
            n_col = self.n_f if df == 0 else REACH
            n_row = self.n_t if dt == 0 else REACH
            here = (r >= 0) & (r < n_row * n_col)
            t0 = 0 if dt == 0 else (-REACH if dt < 0 else self.n_t)
            f0 = 0 if df == 0 else (-REACH if df < 0 else self.n_f)
            time = jnp.where(here, t0 + r // n_col, time)
            freq = jnp.where(here, f0 + r % n_col, freq)
        return time, freq


def window_bias(lay):
    t0 = lax.axis_index("tm") * lay.n_t
    f0 = lax.axis_index("freq") * lay.n_f
    parts = []
    for half in range(2):
        own = half * (lay.own // 2) + jnp.arange(lay.own // 2)[:, None]
        cols = lay.reach(half)
        key_t, key_f = lay.place(jnp.arange(cols.start, cols.stop))
        inside = (
            (t0 + key_t >= 0)
            & (t0 + key_t < lay.n_t * lax.axis_size("tm"))
            & (f0 + key_f >= 0)
            & (f0 + key_f < lay.n_f * lax.axis_size("freq"))
        )
        ok = (
            (jnp.abs(key_t[None] - own // lay.n_f) <= REACH)
            & (jnp.abs(key_f[None] - own % lay.n_f) <= REACH)
            & inside[None]
        )
        parts.append(jnp.where(ok, 0.0, FAR).astype(F32))
    return jnp.stack(parts)


def opposite(side):
    return (-side[0], -side[1])


class Neighbours:
    def __init__(self):
        self.tm, self.fq = lax.axis_index("tm"), lax.axis_index("freq")
        self.t_size, self.f_size = lax.axis_size("tm"), lax.axis_size("freq")

    def exists(self, side):
        t, f = self.tm + side[0], self.fq + side[1]
        return (t >= 0) & (t < self.t_size) & (f >= 0) & (f < self.f_size)

    def device(self, side):
        return ((self.tm + side[0] + self.t_size) % self.t_size, (self.fq + side[1] + self.f_size) % self.f_size)

    def greet(self):
        barrier = pltpu.get_barrier_semaphore()
        for side in SIDES:

            @pl.when(self.exists(side))
            def _(side=side):
                pl.semaphore_signal(barrier, inc=1, device_id=self.device(side), device_id_type=MESH)

        pl.semaphore_wait(barrier, sum(self.exists(side).astype(jnp.int32) for side in SIDES))


class Exchange:
    def __init__(self, lay, near, source, send_sem, recv_sem):
        self.near, self.lay, self.nb = near, lay, Neighbours()
        self.source, self.send_sem, self.recv_sem = source, send_sem, recv_sem

    def copy(self, i):
        side = SIDES[i]
        to = self.lay.region(opposite(side))
        return pltpu.make_async_remote_copy(
            src_ref=self.source(side),
            dst_ref=self.near.at[pl.ds(to.start, to.stop - to.start)],
            send_sem=self.send_sem.at[i],
            recv_sem=self.recv_sem.at[i],
            device_id=self.nb.device(side),
            device_id_type=MESH,
        )

    def start(self):
        for i, side in enumerate(SIDES):

            @pl.when(self.nb.exists(side))
            def _(i=i):
                self.copy(i).start()

    def clear(self):
        for side in SIDES:

            @pl.when(jnp.logical_not(self.nb.exists(side)))
            def _(side=side):
                rows = self.lay.region(side)
                self.near[rows, :] = jnp.zeros((rows.stop - rows.start, self.near.shape[1]), self.near.dtype)

    def arrive(self):
        for i, side in enumerate(SIDES):

            @pl.when(self.nb.exists(opposite(side)))
            def _(i=i):
                self.copy(i).wait_recv()

    def sent(self):
        for i, side in enumerate(SIDES):

            @pl.when(self.nb.exists(side))
            def _(i=i):
                self.copy(i).wait_send()


def edge_source(lay, flat, sides, corners):
    n = REACH * lay.n_f

    def source(side):
        dt, df = side
        if df == 0:
            return flat.at[pl.ds(0 if dt < 0 else lay.own - n, n)]
        if dt == 0:
            return sides.at[0 if df < 0 else 1]
        return corners.at[(dt + 1) + (df + 1) // 2]

    return source


def project_kernel(lay, *refs):
    tok, tok_s, tok_c, grad, grad_s, grad_c, wq, wk, wv, wo = refs[:10]
    q_ref, k_ref, v_ref, g_ref, hid_ref, side_ref, corner_ref = refs[10:17]
    near_tok, hidden, wq_v, wk_v, wv_v, wo_v, w_sem, s_tok, r_tok = refs[17:]
    Neighbours().greet()
    toks = Exchange(lay, near_tok, edge_source(lay, tok, tok_s, tok_c), s_tok, r_tok)
    toks.start()
    loads = [
        pltpu.make_async_copy(src, dst, w_sem.at[i])
        for i, (src, dst) in enumerate(((wq, wq_v), (wk, wk_v), (wv, wv_v), (wo, wo_v)))
    ]
    for load in loads:
        load.start()
    toks.clear()
    side_ref[...] = grad_s[...]
    corner_ref[...] = grad_c[...]

    def normalize(src, shift, start, stop):
        @pl.loop(0, (stop - start) // 32)
        def _(i):
            at = pl.multiple_of(start + i * 32, 32)
            wide = src[pl.ds(pl.multiple_of(at - shift, 32), 32), :].astype(F32)
            center = jnp.mean(wide, axis=-1, keepdims=True)
            shifted = wide - center
            inverse = lax.rsqrt(jnp.mean(shifted * shifted, axis=-1, keepdims=True) + EPS)
            hidden[pl.ds(at, 32), :] = (shifted * inverse).astype(BF16)

    a, b = lay.start, lay.start + lay.own
    normalize(tok, a, a, b)
    hid_ref[...] = hidden[a:b, :]
    for load in loads:
        load.wait()

    def rows(start, stop):
        for dst, w in ((q_ref, wq_v), (k_ref, wk_v), (v_ref, wv_v)):
            dst[start:stop, :] = nn(hidden[start:stop, :], w[...]).astype(BF16)

    rows(a, b)
    g_ref[...] = nt(grad[...], wo_v[...]).astype(BF16)
    toks.arrive()
    for start, stop in ((0, a), (b, lay.all)):
        normalize(near_tok, 0, start, stop)
        rows(start, stop)
    toks.sent()


def strips(lay, m):
    n_t, n_f, model = m.shape
    sides = jnp.stack([m[:, :REACH], m[:, n_f - REACH :]]).reshape(2, REACH * n_t, model)
    corners = jnp.stack(
        [m[t, f].reshape(REACH * REACH, model) for t in (slice(0, REACH), slice(n_t - REACH, n_t))
         for f in (slice(0, REACH), slice(n_f - REACH, n_f))]
    )
    return sides, jnp.pad(corners, ((0, 0), (0, lay.corner - REACH * REACH), (0, 0)))


def project(lay, tokens, d_out, weights):
    model = tokens.shape[-1]
    vm, any_ = pl.BlockSpec(memory_space=pltpu.VMEM), pl.BlockSpec(memory_space=pl.ANY)
    ext = jax.ShapeDtypeStruct((lay.all, model), BF16)
    grad_strips = strips(lay, d_out)
    sem = pltpu.SemaphoreType.DMA((len(SIDES),))
    return pl.pallas_call(
        functools.partial(project_kernel, lay),
        out_shape=[ext] * 3
        + [jax.ShapeDtypeStruct((lay.own, model), BF16)] * 2
        + [jax.ShapeDtypeStruct(a.shape, BF16) for a in grad_strips],
        in_specs=[vm] * 6 + [any_] * 4,
        out_specs=[vm] * 7,
        scratch_shapes=[pltpu.VMEM((lay.all, model), BF16)] * 2
        + [pltpu.VMEM(w.shape, BF16) for w in weights]
        + [pltpu.SemaphoreType.DMA((4,))]
        + [sem] * 2,
        compiler_params=pltpu.CompilerParams(
            collective_id=2, has_side_effects=True, vmem_limit_bytes=48 * 1024 * 1024
        ),
    )(
        tokens.reshape(lay.own, model),
        *strips(lay, tokens),
        d_out.reshape(lay.own, model),
        *grad_strips,
        *weights,
    )


def stats_kernel(lay, stat, att, tok, wo, own_g, far, near_ref, out_ref, g_ref, near, sides, corners, s_sem, r_sem):
    n_t, n_f = lay.n_t, lay.n_f
    Neighbours().greet()
    corners[...] = jnp.zeros(corners.shape, F32)
    for t in range(n_t):
        sides[0, t * REACH : (t + 1) * REACH, :] = stat[t * n_f : t * n_f + REACH, :]
        sides[1, t * REACH : (t + 1) * REACH, :] = stat[(t + 1) * n_f - REACH : (t + 1) * n_f, :]
    for j, first in enumerate((0, n_t - REACH)):
        for r in range(REACH):
            at = (first + r) * n_f
            corners[2 * j, r * REACH : (r + 1) * REACH, :] = stat[at : at + REACH, :]
            corners[2 * j + 1, r * REACH : (r + 1) * REACH, :] = stat[at + n_f - REACH : at + n_f, :]
    ex = Exchange(lay, near, edge_source(lay, stat, sides, corners), s_sem, r_sem)
    ex.start()
    ex.clear()
    near[lay.region((0, 0)), :] = stat[...]
    out_ref[...] = (tok[...].astype(F32) + nn(att[...], wo[...])).astype(BF16)
    a, b = lay.start, lay.start + lay.own
    g_ref[:a, :] = nt(far[:a, :], wo[...]).astype(BF16)
    g_ref[a:b, :] = own_g[...]
    g_ref[b:, :] = nt(far[b:, :], wo[...]).astype(BF16)
    ex.arrive()
    for half in range(2):
        near_ref[half] = near[lay.reach(half), :].T
    ex.sent()


def exchange_stats(lay, stats, attended, flat, w_out, grad_att, far):
    vm = pl.BlockSpec(memory_space=pltpu.VMEM)
    sem = pltpu.SemaphoreType.DMA((len(SIDES),))
    return pl.pallas_call(
        functools.partial(stats_kernel, lay),
        out_shape=[
            jax.ShapeDtypeStruct((2, 128, lay.span), F32),
            jax.ShapeDtypeStruct(flat.shape, BF16),
            jax.ShapeDtypeStruct(far.shape, BF16),
        ],
        in_specs=[vm] * 6,
        out_specs=[vm] * 3,
        scratch_shapes=[
            pltpu.VMEM((lay.all, 128), F32),
            pltpu.VMEM((2, REACH * lay.n_t, 128), F32),
            pltpu.VMEM((4, lay.corner, 128), F32),
            sem,
            sem,
        ],
        compiler_params=pltpu.CompilerParams(
            collective_id=3, has_side_effects=True, vmem_limit_bytes=24 * 1024 * 1024
        ),
    )(stats, attended, flat, w_out, grad_att, far)


def log2(n):
    return n.bit_length() - 1


def axis_orders(t_size, f_size):
    rest = [("freq", b) for b in range(log2(f_size))] + [("tm", b) for b in range(1, log2(t_size))]
    head, last = rest[:-1], rest[-1:]
    turns = [head[i:] + head[:i] for i in (2, 1, 0)] + [[head[1], head[0]] + head[2:]]
    return [[("tm", 0)] + turn + last for turn in turns]


def scatter_kernel(orders, sizes, scale, lay, width, *refs):
    n_mat = len(orders)
    n_st = len(orders[0])
    lefts = refs[:n_mat]
    gq_ref, do_ref = refs[n_mat : n_mat + 2]
    key_ins = refs[n_mat + 2 : n_mat + 8]
    out_ref, gk_ref, gv_ref, total = refs[n_mat + 8 : n_mat + 12]
    rights = (gq_ref, gk_ref, gv_ref, do_ref)
    sends = refs[n_mat + 12 : n_mat + 12 + n_st]
    lands = refs[n_mat + 12 + n_st : n_mat + 12 + 2 * n_st]
    send_sem, recv_sem = refs[-2:]
    tm, fq = lax.axis_index("tm"), lax.axis_index("freq")

    def bit(dim):
        axis, b = dim
        return ((tm if axis == "tm" else fq) // (1 << b)) % 2

    def partner(dim):
        axis, b = dim
        move = (1 - 2 * bit(dim)) * (1 << b)
        return (tm + move, fq) if axis == "tm" else (tm, fq + move)

    barrier = pltpu.get_barrier_semaphore()
    for dim in orders[0]:
        pl.semaphore_signal(barrier, inc=1, device_id=partner(dim), device_id_type=MESH)
    pl.semaphore_wait(barrier, n_st)

    def copy(m, st):
        return pltpu.make_async_remote_copy(
            src_ref=sends[st].at[m],
            dst_ref=lands[st].at[m],
            send_sem=send_sem.at[m, st],
            recv_sem=recv_sem.at[m, st],
            device_id=partner(orders[m][st]),
            device_id_type=MESH,
        )

    base = [0] * n_mat

    def begin(m):
        half = sizes[0]
        theirs = pl.multiple_of((1 - bit(orders[m][0])) * half, half)
        sends[0][m] = nn(lefts[m][pl.ds(theirs, half), :], rights[m][...]).astype(BF16)
        copy(m, 0).start()

    def own_part(m):
        half = sizes[0]
        mine = pl.multiple_of(bit(orders[m][0]) * half, half)
        total[m] = nn(lefts[m][pl.ds(mine, half), :], rights[m][...])

    def advance(m, st):
        half = sizes[st]
        copy(m, st - 1).wait()
        b = bit(orders[m][st])
        theirs, mine = (1 - b) * half, b * half
        if half >= 16:
            theirs, mine = pl.multiple_of(theirs, half), pl.multiple_of(mine, half)
            there = pl.multiple_of(base[m] + theirs, half)
            here = pl.multiple_of(base[m] + mine, half)
            away = total[m, pl.ds(there, half), :] + lands[st - 1][m, pl.ds(theirs, half), :].astype(F32)
            sends[st][m] = away.astype(BF16)
            copy(m, st).start()
            total[m, pl.ds(here, half), :] += lands[st - 1][m, pl.ds(mine, half), :].astype(F32)
        else:
            start = pl.multiple_of(base[m], 2 * half)
            both = total[m, pl.ds(start, 2 * half), :] + lands[st - 1][m].astype(F32)
            low, high = both[:half], both[half:]
            away = jnp.where(b == 0, high, low)
            sends[st][m] = jnp.concatenate([away, away], axis=0).astype(BF16)
            copy(m, st).start()
            here = pl.multiple_of(base[m] + mine, half)
            total[m, pl.ds(here, half), :] = jnp.where(b == 0, low, high)
        base[m] = here

    early, late = (n_mat - 1, 0), (1, 2)
    turn = early + late
    for m in early:
        begin(m)
    for m in early:
        own_part(m)
    for m in early:
        advance(m, 1)
    key_pass(scale, lay, width, *key_ins, gk_ref, gv_ref)
    for m in late:
        begin(m)
    for m in early:
        advance(m, 2)
    for m in late:
        own_part(m)
    for m in late:
        advance(m, 1)
    for st in range(2, n_st):
        for m in early:
            if st + 1 < n_st:
                advance(m, st + 1)
        for m in late:
            advance(m, st)
    half = sizes[-1]
    for m in turn:
        copy(m, n_st - 1).wait()
        out_ref[m] = total[m, pl.ds(base[m], half), :] + lands[-1][m].astype(F32)[0:half]


def scatter_sum(lefts, grad_query, d_out, key_ins, lay, width, t_size, f_size):
    n_dev = t_size * f_size
    n_st = log2(n_dev)
    orders = axis_orders(t_size, f_size)
    tokens, model = lefts[0].shape
    rows = model // n_dev
    sizes = [model >> (s + 1) for s in range(n_st)]
    flipped = []
    for left, order in zip(lefts, orders):
        place = [
            log2(t_size) - 1 - b if axis == "tm" else log2(t_size) + log2(f_size) - 1 - b for axis, b in order
        ]
        cube = left.T.reshape((2,) * n_st + (rows, tokens))
        flipped.append(cube.transpose(place + [n_st, n_st + 1]).reshape(model, tokens))
    n_mat = len(orders)
    blocks = [(n_mat, max(s, 16), model) for s in sizes]
    vm = pl.BlockSpec(memory_space=pltpu.VMEM)
    return pl.pallas_call(
        functools.partial(scatter_kernel, orders, sizes, 1.0 / math.sqrt(width), lay, width),
        out_shape=[jax.ShapeDtypeStruct((n_mat, rows, model), F32)]
        + [jax.ShapeDtypeStruct((tokens, model), BF16)] * 2,
        in_specs=[vm] * (n_mat + 8),
        out_specs=[vm] * 3,
        scratch_shapes=[pltpu.VMEM((n_mat, sizes[0], model), F32)]
        + [pltpu.VMEM(b, BF16) for b in blocks]
        + [pltpu.VMEM(b, BF16) for b in blocks]
        + [pltpu.SemaphoreType.DMA((n_mat, n_st)), pltpu.SemaphoreType.DMA((n_mat, n_st))],
        compiler_params=pltpu.CompilerParams(
            collective_id=1, has_side_effects=True, vmem_limit_bytes=56 * 1024 * 1024
        ),
        cost_estimate=pl.CostEstimate(
            flops=2 * n_mat * tokens * model * model, bytes_accessed=4 * tokens * model, transcendentals=0
        ),
    )(*flipped, grad_query, d_out, *key_ins)


def layer_norm(flat_rows):
    wide = flat_rows.astype(F32)
    center = jnp.mean(wide, axis=-1, keepdims=True)
    shifted = wide - center
    inverse = lax.rsqrt(jnp.mean(shifted * shifted, axis=-1, keepdims=True) + EPS)
    return shifted * inverse, inverse


def local(tokens, w_query, w_key, w_value, w_out, d_out):
    n_t, n_f, model = tokens.shape
    lay = Layout(n_t, n_f)
    flat = tokens.reshape(lay.own, model)
    grad_flat = d_out.reshape(lay.own, model)
    normed, inverse = layer_norm(flat)
    bias = window_bias(lay)
    query, key, value, grad_att, hidden, g_sides, g_corners = project(lay, tokens, d_out, (w_query, w_key, w_value, w_out))
    first = attention_calls(lay, model // HEADS, model)
    attended, grad_query, stats, far = first(query, grad_att, key, value, bias, grad_flat, g_sides, g_corners)
    near_stats, output, near_gatt = exchange_stats(lay, stats, attended, flat, w_out, grad_att, far)
    weight_grads, grad_key, grad_value = scatter_sum(
        [hidden, hidden, hidden, attended],
        grad_query,
        grad_flat,
        (key, value, query, near_gatt, bias, near_stats),
        lay,
        model // HEADS,
        lax.axis_size("tm"),
        lax.axis_size("freq"),
    )
    weight_grads = weight_grads.transpose(1, 0, 2)

    grad_hidden = nt(grad_query, w_query) + nt(grad_key, w_key) + nt(grad_value, w_value)
    center = jnp.mean(grad_hidden, axis=-1, keepdims=True)
    along = jnp.mean(grad_hidden * normed, axis=-1, keepdims=True)
    input_grad = (grad_flat.astype(F32) + (grad_hidden - center - normed * along) * inverse).astype(BF16)
    return output.reshape(n_t, n_f, model), input_grad.reshape(n_t, n_f, model), weight_grads


def solution(mesh):
    tile = P("tm", "freq", None)
    in_specs = (tile, P(), P(), P(), P(), tile)
    out_specs = (tile, tile, P(("tm", "freq"), None, None))
    return jax.shard_map(local, mesh=mesh, in_specs=in_specs, out_specs=out_specs, check_vma=False)
```
